256 devices in a mesh: dp: 8 (over y, z_hi), mp: 32 (over x, z_lo, core).
Axes of the slice: x: 4, y: 4, z: 8 (z_hi: 2, z_lo: 4; z = z_hi * 4 + z_lo), core: 2. Of those that a mesh axis runs over, the one named last changes fastest.
Arguments:
- tokens: bfloat16 [8192, 4608], P(('dp', 'mp')), parts along dimension 0, may hold values from -4 to 4
- ln_gain: float32 [4608], replicated, may hold values from 0.5 to 1.5
- w_qkv: bfloat16 [4608, 3, 4096], P(None, None, 'mp'), may hold values from -0.09375 to 0.09375
- q_gain: float32 [128], replicated, may hold values from 0.8 to 2.4
- k_gain: float32 [128], replicated, may hold values from 0.8 to 2.4
- w_up: bfloat16 [4608, 12288], P(None, 'mp'), may hold values from -0.09375 to 0.09375
- up_bias: float32 [12288], P('mp'), may hold values from -3 to 3
- w_out_attn: bfloat16 [4096, 4608], P('mp'), may hold values from -0.375 to 0.375
- w_down: bfloat16 [12288, 4608], P('mp'), may hold values from -0.0546875 to 0.0546875
Outputs:
- layer_out: bfloat16 [8192, 4608], P(('dp', 'mp')), parts along dimension 0
The draws below stay inside these ranges and needn't reach their ends.
There are 8 independent parts, one for each index of `dp`. The reference program is written for one: setup_inputs(seed, part) draws one part's arguments, and reference() takes and returns one part's arrays. A program takes and returns all parts, laid end to end along the dimension named above; an argument that names none is the same for every part. Nothing has to cross between parts.
All inputs are finite; a program needn't handle non-finite values.
Results may differ from the reference program's by a relative error of at most 0.03.
Values may be sent and summed in bfloat16 or wider, within the bound.
No kernel may reach another device: no remote copies, remote signals or barrier semaphores. Data moves between devices by JAX's collectives and lax.ppermute only.
A program may use at most 128 MiB of HBM per device.

```python
import math
import jax
import jax.numpy as jnp
from jax import lax

D = 4608
FF = 12288
HEADS = 32
HEAD_DIM = 128
PATCHES = 256
TOKENS = 1024


def block_levels(stream_key, shape, shards, least, top_value):
    level = 1.0
    for axis_at, blocks in shards:
        heights = jax.random.uniform(jax.random.fold_in(jax.random.fold_in(stream_key, 6), axis_at), (blocks,), jnp.float32, least / len(shards), top_value / len(shards))
        level = level * jnp.repeat(jnp.exp(heights), shape[axis_at] // blocks).reshape((-1,) + (1,) * (len(shape) - 1 - axis_at))
    return level


def gaussian(rng, shape, deviation, most, cuts=(), kind=jnp.bfloat16):
    values = jax.random.normal(rng, shape, jnp.float32) * deviation
    if len(cuts) > 0:
        values = block_levels(rng, shape, cuts, -0.22, 0.18) * values
    return jnp.clip(values, min=-most, max=most).astype(kind)


def setup_inputs(seed: int = 0, part: int = 0) -> dict:
    arg_keys = jax.random.split(jax.random.key(seed), 10)
    part_keys = jax.random.split(jax.random.fold_in(arg_keys[9], part), 10)
    tokens = gaussian(part_keys[0], (TOKENS, D), 0.5, 4.0, ((0, 32),))
    ln_gain = jnp.clip(jax.random.uniform(arg_keys[1], (D,), jnp.float32, 0.5, 1.5), 0.5, 1.5)
    w_qkv = gaussian(arg_keys[2], (D, 3, HEADS * HEAD_DIM), D ** -0.5, 0.09375, ((2, 32),))
    q_gain = jnp.clip(jax.random.uniform(arg_keys[3], (HEAD_DIM,), jnp.float32, 0.8, 2.4), 0.8, 2.4)
    k_gain = jnp.clip(jax.random.uniform(arg_keys[4], (HEAD_DIM,), jnp.float32, 0.8, 2.4), 0.8, 2.4)
    w_up = gaussian(arg_keys[5], (D, FF), D ** -0.5, 0.09375, ((1, 32),))
    up_bias = gaussian(arg_keys[6], (FF,), 0.5, 3.0, ((0, 32),), jnp.float32)
    w_out_attn = gaussian(arg_keys[7], (HEADS * HEAD_DIM, D), (HEADS * HEAD_DIM // 16) ** -0.5, 0.375, ((0, 32),))
    w_down = gaussian(arg_keys[8], (FF, D), FF ** -0.5, 0.0546875, ((0, 32),))
    return {"tokens": tokens, "ln_gain": ln_gain, "w_qkv": w_qkv, "q_gain": q_gain, "k_gain": k_gain, "w_up": w_up, "up_bias": up_bias, "w_out_attn": w_out_attn, "w_down": w_down}


def normalize(rows, gain):
    values = rows.astype(jnp.float32)
    mean = lax.optimization_barrier(jnp.mean(values, axis=-1, keepdims=True))
    centred = values - mean
    spread = lax.optimization_barrier(jnp.mean(centred * centred, axis=-1, keepdims=True))
    return centred * jax.lax.rsqrt(spread + 1e-06) * gain

def reference(tokens, ln_gain, w_qkv, q_gain, k_gain, w_up, up_bias, w_out_attn, w_down):
    count = tokens.shape[0]
    width = w_qkv.shape[2]
    heads = width // HEAD_DIM
    images = count // PATCHES
    normed = normalize(tokens, ln_gain).astype(jnp.bfloat16)
    joined = jnp.einsum('td,dcf->tcf', normed.astype(jnp.float32), w_qkv.astype(jnp.float32))
    query = normalize(joined[:, 0].reshape(count, heads, HEAD_DIM), q_gain).astype(jnp.bfloat16)
    key = normalize(joined[:, 1].reshape(count, heads, HEAD_DIM), k_gain).astype(jnp.bfloat16)
    value = joined[:, 2].reshape(count, heads, HEAD_DIM).astype(jnp.bfloat16)
    query = query.reshape(images, PATCHES, heads, HEAD_DIM).astype(jnp.float32)
    key = key.reshape(images, PATCHES, heads, HEAD_DIM).astype(jnp.float32)
    value = value.reshape(images, PATCHES, heads, HEAD_DIM).astype(jnp.float32)
    scores = jnp.einsum('iphe,iqhe->ihpq', query, key) / math.sqrt(HEAD_DIM)
    expo = jnp.exp(scores)
    weights = (expo / lax.optimization_barrier(jnp.sum(expo, axis=-1, keepdims=True))).astype(jnp.bfloat16)
    attended = jnp.einsum('ihpq,iqhe->iphe', weights.astype(jnp.float32), value)
    attended = attended.astype(jnp.bfloat16).reshape(count, width)
    hidden = jax.nn.gelu(jnp.dot(normed, w_up, preferred_element_type=jnp.float32) + up_bias).astype(jnp.bfloat16)
    total = jnp.dot(attended, w_out_attn, preferred_element_type=jnp.float32) + jnp.dot(hidden, w_down, preferred_element_type=jnp.float32)
    return (tokens.astype(jnp.float32) + total).astype(jnp.bfloat16)
```

```python
import math

import jax
import jax.numpy as jnp
from jax import lax
from jax.sharding import PartitionSpec as P

HEAD_DIM = 128
PATCHES = 256
NX = 4
NZ = 4
RING = (1, 2, 3, 0)
BF16 = jnp.bfloat16
F32 = jnp.float32


def moves(dx, dz, dc):
    pairs = []
    for x in range(NX):
        for z in range(NZ):
            for c in range(2):
                to = (((x + dx) % NX) * NZ + (z + dz) % NZ) * 2 + (c + dc) % 2
                pairs.append(((x * NZ + z) * 2 + c, to))
    return pairs


RIGHT = moves(1, 0, 0)
LEFT = moves(-1, 0, 0)
UP = moves(0, 1, 0)
TWIN = moves(0, 0, 1)


def send(rows, way):
    return lax.ppermute(rows, "mp", way)


def normalize(rows, gain):
    values = rows.astype(F32)
    mean = jnp.mean(values, axis=-1, keepdims=True)
    centred = values - mean
    spread = jnp.mean(centred * centred, axis=-1, keepdims=True)
    return centred * lax.rsqrt(spread + 1e-06) * gain


def gather_block(block):
    half = block.shape[0] // 2
    from_left = send(block, RIGHT)
    from_right = send(block, LEFT)
    far_top = send(from_left[:half], RIGHT)
    far_bottom = send(from_right[half:], LEFT)
    mine = [block, from_left, from_right, far_top, far_bottom]
    pieces = []
    for piece in mine[:3]:
        pieces += [piece, send(piece, TWIN)]
    pieces += [far_top, far_bottom, send(far_top, TWIN), send(far_bottom, TWIN)]
    return jnp.concatenate(pieces, axis=0)


def attend(query, key_rows, value):
    scores = jnp.einsum("ipe,iqe->ipq", query, key_rows, preferred_element_type=F32)
    expo = jnp.exp(scores / math.sqrt(HEAD_DIM))
    weights = (expo / jnp.sum(expo, axis=-1, keepdims=True)).astype(BF16)
    return jnp.einsum("ipq,iqe->ipe", weights, value, preferred_element_type=F32).astype(BF16)


def reduce_block(partial):
    half = partial.shape[2] // 2
    mine = partial[:, 0].astype(F32) + send(partial[:, 1], TWIN).astype(F32)
    top = send(mine[3, :half].astype(BF16), RIGHT).astype(F32)
    bottom = send(mine[3, half:].astype(BF16), LEFT).astype(F32)
    to_right = jnp.concatenate([mine[2, :half] + top, mine[2, half:]], axis=0).astype(BF16)
    to_left = jnp.concatenate([mine[1, :half], mine[1, half:] + bottom], axis=0).astype(BF16)
    return mine[0] + send(to_right, RIGHT).astype(F32) + send(to_left, LEFT).astype(F32)


def shards(tokens, ln_gain, w_qkv, q_gain, k_gain, w_up, up_bias, w_out_attn, w_down):
    depth = tokens.shape[1]
    rows = tokens.shape[0]
    w_in = jnp.concatenate([w_qkv.reshape(depth, 3 * HEAD_DIM), w_up], axis=1)
    w_out = jnp.concatenate([w_out_attn, w_down], axis=0)
    normed = normalize(tokens, ln_gain).astype(BF16)

    blocks = [normed]
    for _ in range(NZ - 1):
        blocks.append(send(blocks[-1], UP))
    query, key_rows, value, hidden = [], [], [], []
    for block in blocks:
        joined = jnp.dot(gather_block(block), w_in, preferred_element_type=F32)
        query.append(normalize(joined[:, :HEAD_DIM], q_gain).astype(BF16))
        key_rows.append(normalize(joined[:, HEAD_DIM : 2 * HEAD_DIM], k_gain).astype(BF16))
        value.append(joined[:, 2 * HEAD_DIM : 3 * HEAD_DIM].astype(BF16))
        hidden.append(jax.nn.gelu(joined[:, 3 * HEAD_DIM :] + up_bias).astype(BF16))

    def by_image(parts):
        return jnp.concatenate([p.reshape(NX, 2 * rows, HEAD_DIM) for p in parts], axis=1)

    attended = attend(by_image(query), by_image(key_rows), by_image(value))
    attended = attended.reshape(NX, NZ, 2 * rows, HEAD_DIM)

    carried = None
    for k in RING:
        left = jnp.concatenate([attended[:, k].reshape(NX * 2 * rows, HEAD_DIM), hidden[k]], axis=1)
        partial = jnp.dot(left, w_out, preferred_element_type=F32).astype(BF16)
        total = reduce_block(partial.reshape(NX, 2, rows, depth))
        if carried is not None:
            total = total + carried
        if k != 0:
            carried = send(total.astype(BF16), UP).astype(F32)
    return (tokens.astype(F32) + total).astype(BF16)


def solution(mesh):
    placed = (
        P(("dp", "mp"), None),
        P(),
        P(None, None, "mp"),
        P(),
        P(),
        P(None, "mp"),
        P("mp"),
        P("mp", None),
        P("mp", None),
    )
    return jax.shard_map(
        shards, mesh=mesh, in_specs=placed, out_specs=P(("dp", "mp"), None), check_vma=False
    )
```

```python
import functools
import math

import jax
import jax.numpy as jnp
from jax import lax
from jax.experimental import pallas as pl
from jax.experimental.pallas import tpu as pltpu
from jax.sharding import PartitionSpec as P

HEAD_DIM = 128
NX = 4
NZ = 4
BF16 = jnp.bfloat16
F32 = jnp.float32
MIB = 1 << 20


def moves(dx, dz, dc):
    pairs = []
    for x in range(NX):
        for z in range(NZ):
            for c in range(2):
                to = (((x + dx) % NX) * NZ + (z + dz) % NZ) * 2 + (c + dc) % 2
                pairs.append(((x * NZ + z) * 2 + c, to))
    return pairs


RIGHT = moves(1, 0, 0)
LEFT = moves(-1, 0, 0)
UP = moves(0, 1, 0)
TWIN = moves(0, 0, 1)


def send(rows, way):
    return lax.ppermute(rows, "mp", way)


def whole(count):
    return [pl.BlockSpec(memory_space=pltpu.VMEM)] * count


def dot(a, b):
    return jnp.dot(a, b, preferred_element_type=F32)


def normalize(rows, gain):
    values = rows.astype(F32)
    mean = jnp.mean(values, axis=-1, keepdims=True)
    centred = values - mean
    spread = jnp.mean(centred * centred, axis=-1, keepdims=True)
    return centred * lax.rsqrt(spread + 1e-06) * gain


def norm_kernel(rows_ref, gain_ref, out_ref):
    out_ref[...] = normalize(rows_ref[...], gain_ref[...].reshape(1, -1)).astype(BF16)


def norm_rows(tokens, gain):
    return pl.pallas_call(
        norm_kernel, out_shape=jax.ShapeDtypeStruct(tokens.shape, BF16)
    )(tokens, gain)


def copy_kernel(skipped, *refs):
    refs = refs[skipped:]
    count = len(refs) // 2
    for i in range(count):
        refs[count + i][...] = refs[i][...]


def after(first, *arrays):
    count = len(arrays)
    return pl.pallas_call(
        functools.partial(copy_kernel, len(first)),
        in_specs=[pl.BlockSpec(memory_space=pl.ANY)] * len(first) + whole(count),
        out_specs=whole(count),
        out_shape=[jax.ShapeDtypeStruct(a.shape, a.dtype) for a in arrays],
        compiler_params=pltpu.CompilerParams(vmem_limit_bytes=12 * MIB),
        cost_estimate=pl.CostEstimate(
            flops=0, bytes_accessed=sum(4 * a.size for a in arrays), transcendentals=0
        ),
    )(*first, *arrays)


def nothing_kernel(*_):
    pass


def gate(array, *first):
    return pl.pallas_call(
        nothing_kernel,
        in_specs=[pl.BlockSpec(memory_space=pl.ANY)] * (1 + len(first)),
        out_specs=pl.BlockSpec(memory_space=pl.ANY),
        out_shape=jax.ShapeDtypeStruct(array.shape, array.dtype),
        input_output_aliases={0: 0},
        compiler_params=pltpu.CompilerParams(vmem_limit_bytes=MIB),
        cost_estimate=pl.CostEstimate(flops=0, bytes_accessed=0, transcendentals=0),
    )(array, *first)


def project_kernel(count, *refs):
    pieces, rest = refs[:count], refs[count:]
    qkv_own, qkv_twin, up_own, up_twin, q_gain, k_gain, bias_own, bias_twin = rest[:8]
    query, key_value, hidden, rows = rest[8:]
    size = pieces[0].shape[0]
    head = HEAD_DIM
    for i, piece in enumerate(pieces):
        rows[pl.ds(i * size, size), :] = piece[...]
    for t, (qkv, up, bias_ref) in enumerate(
        ((qkv_own, up_own, bias_own), (qkv_twin, up_twin, bias_twin))
    ):
        bias = bias_ref[...].reshape(1, -1)
        first = dot(rows[...], jnp.concatenate([qkv[0], qkv[1]], axis=1))
        query[:, t * head : (t + 1) * head] = normalize(
            first[:, :head], q_gain[...].reshape(1, -1)
        ).astype(BF16)
        at = 2 * t * head
        key_value[:, at : at + head] = normalize(
            first[:, head:], k_gain[...].reshape(1, -1)
        ).astype(BF16)
        second = dot(rows[...], jnp.concatenate([qkv[2], up[:, :head]], axis=1))
        key_value[:, at + head : at + 2 * head] = second[:, :head].astype(BF16)
        at = 3 * t * head
        hidden[:, at : at + head] = jax.nn.gelu(second[:, head:] + bias[:, :head]).astype(BF16)
        third = dot(rows[...], up[:, head:])
        hidden[:, at + head : at + 3 * head] = jax.nn.gelu(third + bias[:, head:]).astype(BF16)


def project(pieces, *weights):
    size, depth = pieces[0].shape
    count = len(pieces) * size
    return pl.pallas_call(
        functools.partial(project_kernel, len(pieces)),
        in_specs=whole(len(pieces) + 8),
        out_specs=whole(3),
        out_shape=[jax.ShapeDtypeStruct((count, n * HEAD_DIM), BF16) for n in (2, 4, 6)],
        scratch_shapes=[pltpu.VMEM((count, depth), BF16)],
        compiler_params=pltpu.CompilerParams(vmem_limit_bytes=20 * MIB),
        cost_estimate=pl.CostEstimate(
            flops=24 * count * depth * HEAD_DIM,
            bytes_accessed=24 * depth * HEAD_DIM + 2 * count * depth,
            transcendentals=6 * count * HEAD_DIM,
        ),
    )(*pieces, *weights)


def attend_kernel(count, size, *refs):
    query_refs, own_refs, twin_refs, out_refs = (
        refs[i * count : (i + 1) * count] for i in range(4)
    )

    def image(some, m, at):
        return [
            ref[pl.ds((j * NX + m) * size, size), at : at + HEAD_DIM]
            for ref in some
            for j in range(ref.shape[0] // (NX * size))
        ]

    for m in range(NX):
        for t in range(2):
            own, twin = 2 * t * HEAD_DIM, 2 * (1 - t) * HEAD_DIM
            query = jnp.concatenate(image(query_refs, m, t * HEAD_DIM), axis=0)
            key_rows = jnp.concatenate(image(own_refs, m, own) + image(twin_refs, m, twin), axis=0)
            value = jnp.concatenate(
                image(own_refs, m, own + HEAD_DIM) + image(twin_refs, m, twin + HEAD_DIM), axis=0
            )
            scores = lax.dot_general(
                query, key_rows, (((1,), (1,)), ((), ())), preferred_element_type=F32
            )
            expo = jnp.exp(scores / math.sqrt(HEAD_DIM))
            weights = (expo / jnp.sum(expo, axis=-1, keepdims=True)).astype(BF16)
            mixed = dot(weights, value).astype(BF16)
            at = 0
            for ref in out_refs:
                for j in range(ref.shape[0] // (NX * size)):
                    ref[pl.ds((j * NX + m) * size, size), t * HEAD_DIM : (t + 1) * HEAD_DIM] = mixed[
                        at : at + size
                    ]
                    at += size


def attend(size, query, own, twin):
    return pl.pallas_call(
        functools.partial(attend_kernel, len(query), size),
        in_specs=whole(3 * len(query)),
        out_specs=whole(len(query)),
        out_shape=[jax.ShapeDtypeStruct(a.shape, BF16) for a in query],
        compiler_params=pltpu.CompilerParams(vmem_limit_bytes=12 * MIB),
        cost_estimate=pl.CostEstimate(
            flops=140_000_000, bytes_accessed=2_000_000, transcendentals=270_000
        ),
    )(*query, *own, *twin)


def spread_kernel(start, att, hid, attn_own, attn_twin, down_own, down_twin, *rest):
    outs = rest[-NX:]
    size = outs[0].shape[0]
    left = jnp.concatenate([att[pl.ds(start, NX * size), :], hid[pl.ds(start, NX * size), :]], axis=1)
    right = jnp.concatenate(
        [attn_own[...], attn_twin[...], down_own[...], down_twin[...]], axis=0
    )
    partial = dot(left, right).astype(BF16)
    for m, out in enumerate(outs):
        out[...] = partial[m * size : (m + 1) * size]


def spread(size, start, att, hid, weights, first):
    depth = weights[0].shape[1]
    return pl.pallas_call(
        functools.partial(spread_kernel, start),
        in_specs=whole(6) + [pl.BlockSpec(memory_space=pl.ANY)] * len(first),
        out_specs=whole(NX),
        out_shape=[jax.ShapeDtypeStruct((size, depth), BF16)] * NX,
        compiler_params=pltpu.CompilerParams(vmem_limit_bytes=16 * MIB),
        cost_estimate=pl.CostEstimate(
            flops=16 * NX * size * depth * HEAD_DIM,
            bytes_accessed=16 * depth * HEAD_DIM + 2 * NX * size * depth,
            transcendentals=0,
        ),
    )(att, hid, *weights, *first)


def added(*parts):
    return sum(p.astype(F32) for p in parts).astype(BF16)


def shards(tokens, ln_gain, w_qkv, q_gain, k_gain, w_up, up_bias, w_out_attn, w_down):
    rows, depth = tokens.shape
    w_qkv = jnp.transpose(w_qkv, (1, 0, 2))

    held, left, right, far = {}, {}, {}, {}
    held[0] = norm_rows(tokens, ln_gain)
    left[0] = send(held[0], RIGHT)
    right[0] = send(held[0], LEFT)
    next1 = send(held[0], UP)
    held[1] = gate(next1, left[0], right[0])
    far[0] = send(left[0], RIGHT)
    left[1] = send(held[1], RIGHT)
    right[1] = send(held[1], LEFT)
    far[1] = send(right[1], LEFT)
    held[2] = gate(send(held[1], UP), far[0], right[1], left[1])
    left[2] = send(held[2], RIGHT)
    right[2] = send(held[2], LEFT)
    far[2] = send(left[2], RIGHT)
    next3 = send(held[2], UP)
    held[3] = gate(next3, far[1], left[2])
    left[3] = send(held[3], RIGHT)
    right[3] = send(held[3], LEFT)
    far[3] = send(right[3], LEFT)
    pieces = [[held[k], left[k], right[k], far[k]] for k in range(NZ)]

    up_twin = send(w_up, TWIN)
    qkv_copy, bias_copy = after((up_twin, left[0], right[0], next1), w_qkv, up_bias)
    qkv_twin, bias_twin = send(qkv_copy, TWIN), send(bias_copy, TWIN)
    late = after((qkv_twin, far[1], left[2], right[2], next3), w_down, w_out_attn)
    down_twin, attn_twin = (send(a, TWIN) for a in late)
    w_in = (w_qkv, qkv_twin, w_up, up_twin, q_gain, k_gain, up_bias, bias_twin)
    w_out = (w_out_attn, attn_twin, w_down, down_twin)

    groups = [pieces[0] + pieces[1], pieces[2], pieces[3]]
    query, own, hidden = zip(*[project(group, *w_in) for group in groups])
    twin = [send(part, TWIN) for part in own]
    attended = attend(rows, query, own, twin)

    block_rows = NX * rows
    place = {0: (0, 0), 1: (0, block_rows), 2: (1, 0), 3: (2, 0)}

    def block_sums(k, *first):
        group, start = place[k]
        return spread(rows, start, attended[group], hidden[group], w_out, first)

    mine1, left1, right1, far1 = block_sums(1)
    far1 = send(far1, LEFT)
    from_left1 = send(right1, RIGHT)
    mine2, left2, right2, far2 = block_sums(2, mine1)
    far2 = send(far2, RIGHT)
    from_right1 = send(added(left1, far1), LEFT)
    from_right2 = send(left2, LEFT)
    from_left2 = send(added(right2, far2), RIGHT)
    mine3, left3, right3, far3 = block_sums(3, mine2, far2, far1)
    far3 = send(far3, LEFT)
    from_left3 = send(right3, RIGHT)
    up1 = send(added(mine1, from_left1, from_right1), UP)
    mine0, left0, right0, far0 = block_sums(0, mine3, from_right2, from_left2)
    far0 = send(far0, RIGHT)
    from_right3 = send(added(left3, far3), LEFT)
    up2 = send(added(mine2, from_left2, from_right2, up1), UP)
    from_right0 = send(left0, LEFT)
    from_left0 = send(added(right0, far0), RIGHT)
    up3 = send(added(mine3, from_left3, from_right3, up2), UP)
    return added(tokens, mine0, from_left0, from_right0, up3)


def solution(mesh):
    placed = (
        P(("dp", "mp"), None),
        P(),
        P(None, None, "mp"),
        P(),
        P(),
        P(None, "mp"),
        P("mp"),
        P("mp", None),
        P("mp", None),
    )
    return jax.shard_map(
        shards, mesh=mesh, in_specs=placed, out_specs=P(("dp", "mp"), None), check_vma=False
    )
```

```python
import functools
import math

import jax
import jax.numpy as jnp
from jax import lax
from jax.experimental import pallas as pl
from jax.experimental.pallas import tpu as pltpu
from jax.sharding import PartitionSpec as P

HEAD_DIM = 128
NX = 4
NZ = 4
BF16 = jnp.bfloat16
F32 = jnp.float32
MIB = 1 << 20


Z_NEXT = (1, 3, 0, 2)


def moves(dx, up, dc):
    pairs = []
    for x in range(NX):
        for z in range(NZ):
            for c in range(2):
                to = (((x + dx) % NX) * NZ + (Z_NEXT[z] if up else z)) * 2 + (c + dc) % 2
                pairs.append(((x * NZ + z) * 2 + c, to))
    return pairs


RIGHT = moves(1, False, 0)
LEFT = moves(-1, False, 0)
UP = moves(0, True, 0)
TWIN = moves(0, False, 1)


def send(rows, way):
    return lax.ppermute(rows, "mp", way)


def whole(count):
    return [pl.BlockSpec(memory_space=pltpu.VMEM)] * count


def dot(a, b):
    return jnp.dot(a, b, preferred_element_type=F32)


def normalize(rows, gain):
    values = rows.astype(F32)
    mean = jnp.mean(values, axis=-1, keepdims=True)
    centred = values - mean
    spread = jnp.mean(centred * centred, axis=-1, keepdims=True)
    return centred * lax.rsqrt(spread + 1e-06) * gain


def norm_kernel(rows_ref, gain_ref, out_ref):
    out_ref[...] = normalize(rows_ref[...], gain_ref[...].reshape(1, -1)).astype(BF16)


def norm_rows(tokens, gain):
    return pl.pallas_call(
        norm_kernel, out_shape=jax.ShapeDtypeStruct(tokens.shape, BF16)
    )(tokens, gain)


def pack_kernel(skipped, *refs):
    parts, out = refs[skipped:-1], refs[-1]
    at = 0
    for part in parts:
        if len(part.shape) < len(out.shape):
            count = part.shape[-1] // HEAD_DIM
            for i in range(count):
                out[at + i] = part[:, i * HEAD_DIM : (i + 1) * HEAD_DIM]
        else:
            count = part.shape[0]
            out[pl.ds(at, count)] = part[...]
        at += count


def pack(shape, first, *parts):
    return pl.pallas_call(
        functools.partial(pack_kernel, len(first)),
        in_specs=[pl.BlockSpec(memory_space=pl.ANY)] * len(first) + whole(len(parts)),
        out_specs=pl.BlockSpec(memory_space=pltpu.VMEM),
        out_shape=jax.ShapeDtypeStruct(shape, parts[0].dtype),
        compiler_params=pltpu.CompilerParams(vmem_limit_bytes=20 * MIB),
        cost_estimate=pl.CostEstimate(
            flops=0, bytes_accessed=sum(4 * a.size for a in parts), transcendentals=0
        ),
    )(*first, *parts)


def nothing_kernel(*_):
    pass


def gate(array, *first):
    return pl.pallas_call(
        nothing_kernel,
        in_specs=[pl.BlockSpec(memory_space=pl.ANY)] * (1 + len(first)),
        out_specs=pl.BlockSpec(memory_space=pl.ANY),
        out_shape=jax.ShapeDtypeStruct(array.shape, array.dtype),
        input_output_aliases={0: 0},
        compiler_params=pltpu.CompilerParams(vmem_limit_bytes=MIB),
        cost_estimate=pl.CostEstimate(flops=0, bytes_accessed=0, transcendentals=0),
    )(array, *first)


def project_kernel(count, *refs):
    pieces, rest = refs[:count], refs[count:]
    in_own, in_twin, q_gain, k_gain, bias_own, bias_twin = rest[:6]
    query, key_value, hidden, rows = rest[6:]
    size = pieces[0].shape[0]
    head = HEAD_DIM
    for i, piece in enumerate(pieces):
        rows[pl.ds(i * size, size), :] = piece[...]
    for t, (w_in, bias_ref) in enumerate(((in_own, bias_own), (in_twin, bias_twin))):

        def columns(i):
            return dot(rows[...], jnp.concatenate([w_in[i], w_in[i + 1]], axis=1))

        bias = bias_ref[...].reshape(1, -1)
        first = columns(0)
        query[:, t * head : (t + 1) * head] = normalize(
            first[:, :head], q_gain[...].reshape(1, -1)
        ).astype(BF16)
        at = 2 * t * head
        key_value[:, at : at + head] = normalize(
            first[:, head:], k_gain[...].reshape(1, -1)
        ).astype(BF16)
        second = columns(2)
        key_value[:, at + head : at + 2 * head] = second[:, :head].astype(BF16)
        at = 3 * t * head
        hidden[:, at : at + head] = jax.nn.gelu(second[:, head:] + bias[:, :head]).astype(BF16)
        third = columns(4)
        hidden[:, at + head : at + 3 * head] = jax.nn.gelu(third + bias[:, head:]).astype(BF16)


def project(pieces, *weights):
    size, depth = pieces[0].shape
    count = len(pieces) * size
    return pl.pallas_call(
        functools.partial(project_kernel, len(pieces)),
        in_specs=whole(len(pieces) + 6),
        out_specs=whole(3),
        out_shape=[jax.ShapeDtypeStruct((count, n * HEAD_DIM), BF16) for n in (2, 4, 6)],
        scratch_shapes=[pltpu.VMEM((count, depth), BF16)],
        compiler_params=pltpu.CompilerParams(vmem_limit_bytes=20 * MIB),
        cost_estimate=pl.CostEstimate(
            flops=24 * count * depth * HEAD_DIM,
            bytes_accessed=24 * depth * HEAD_DIM + 2 * count * depth,
            transcendentals=6 * count * HEAD_DIM,
        ),
    )(*pieces, *weights)


def attend_kernel(count, size, *refs):
    query_refs, own_refs, twin_refs, out_refs = (
        refs[i * count : (i + 1) * count] for i in range(4)
    )

    def image(some, m, at):
        return [
            ref[pl.ds((j * NX + m) * size, size), at : at + HEAD_DIM]
            for ref in some
            for j in range(ref.shape[0] // (NX * size))
        ]

    for m in range(NX):
        for t in range(2):
            own, twin = 2 * t * HEAD_DIM, 2 * (1 - t) * HEAD_DIM
            query = jnp.concatenate(image(query_refs, m, t * HEAD_DIM), axis=0)
            key_rows = jnp.concatenate(image(own_refs, m, own) + image(twin_refs, m, twin), axis=0)
            value = jnp.concatenate(
                image(own_refs, m, own + HEAD_DIM) + image(twin_refs, m, twin + HEAD_DIM), axis=0
            )
            scores = lax.dot_general(
                query, key_rows, (((1,), (1,)), ((), ())), preferred_element_type=F32
            )
            expo = jnp.exp(scores / math.sqrt(HEAD_DIM))
            weights = (expo / jnp.sum(expo, axis=-1, keepdims=True)).astype(BF16)
            mixed = dot(weights, value).astype(BF16)
            at = 0
            for ref in out_refs:
                for j in range(ref.shape[0] // (NX * size)):
                    ref[pl.ds((j * NX + m) * size, size), t * HEAD_DIM : (t + 1) * HEAD_DIM] = mixed[
                        at : at + size
                    ]
                    at += size


def attend(size, query, own, twin):
    return pl.pallas_call(
        functools.partial(attend_kernel, len(query), size),
        in_specs=whole(3 * len(query)),
        out_specs=whole(len(query)),
        out_shape=[jax.ShapeDtypeStruct(a.shape, BF16) for a in query],
        compiler_params=pltpu.CompilerParams(vmem_limit_bytes=12 * MIB),
        cost_estimate=pl.CostEstimate(
            flops=140_000_000, bytes_accessed=2_000_000, transcendentals=270_000
        ),
    )(*query, *own, *twin)


def spread_kernel(start, att, hid, out_own, out_twin, *rest):
    outs = rest[-NX:]
    size = outs[0].shape[0]
    head = HEAD_DIM
    span = pl.ds(start, NX * size)
    left = jnp.concatenate(
        [att[span, :head], hid[span, : 3 * head], att[span, head:], hid[span, 3 * head :]], axis=1
    )
    right = jnp.concatenate([out_own[...], out_twin[...]], axis=0)
    partial = dot(left, right).astype(BF16)
    for m, out in enumerate(outs):
        out[...] = partial[m * size : (m + 1) * size]


def spread(size, start, att, hid, weights, first):
    depth = weights[0].shape[1]
    return pl.pallas_call(
        functools.partial(spread_kernel, start),
        in_specs=whole(4) + [pl.BlockSpec(memory_space=pl.ANY)] * len(first),
        out_specs=whole(NX),
        out_shape=[jax.ShapeDtypeStruct((size, depth), BF16)] * NX,
        compiler_params=pltpu.CompilerParams(vmem_limit_bytes=16 * MIB),
        cost_estimate=pl.CostEstimate(
            flops=16 * NX * size * depth * HEAD_DIM,
            bytes_accessed=16 * depth * HEAD_DIM + 2 * NX * size * depth,
            transcendentals=0,
        ),
    )(att, hid, *weights, *first)


def added(*parts):
    return sum(p.astype(F32) for p in parts).astype(BF16)


def shards(tokens, ln_gain, w_qkv, q_gain, k_gain, w_up, up_bias, w_out_attn, w_down):
    rows, depth = tokens.shape
    held, left, right, far = {}, {}, {}, {}
    held[0] = norm_rows(tokens, ln_gain)
    in_own = pack((6, depth, HEAD_DIM), (held[0],), jnp.transpose(w_qkv, (1, 0, 2)), w_up)
    in_twin = send(in_own, TWIN)
    next1 = send(held[0], UP)
    left[0] = send(held[0], RIGHT)
    right[0] = send(held[0], LEFT)
    held[1] = gate(next1, left[0], right[0])
    next2 = send(held[1], UP)
    far[0] = send(left[0], RIGHT)
    right[1] = send(held[1], LEFT)
    left[1] = send(held[1], RIGHT)
    far[1] = send(right[1], LEFT)
    held[2] = gate(next2, far[0], right[1], left[1])
    next3 = send(held[2], UP)
    left[2] = send(held[2], RIGHT)
    right[2] = send(held[2], LEFT)
    far[2] = send(left[2], RIGHT)
    held[3] = gate(next3, far[1], left[2])
    right[3] = send(held[3], LEFT)
    left[3] = send(held[3], RIGHT)
    far[3] = send(right[3], LEFT)
    pieces = [[held[k], left[k], right[k], far[k]] for k in range(NZ)]

    bias_twin = send(pack(up_bias.shape, (left[1],), up_bias), TWIN)
    out_own = pack((4 * HEAD_DIM, depth), (right[2], far[2], right[3], bias_twin), w_out_attn, w_down)
    w_in = (in_own, in_twin, q_gain, k_gain, up_bias, bias_twin)
    w_out = (out_own, send(out_own, TWIN))

    groups = [pieces[0] + pieces[1], pieces[2], pieces[3]]
    query, own, hidden = zip(*[project(group, *w_in) for group in groups])
    twin = [send(part, TWIN) for part in own]
    attended = attend(rows, query, own, twin)

    block_rows = NX * rows
    place = {0: (0, 0), 1: (0, block_rows), 2: (1, 0), 3: (2, 0)}

    def block_sums(k, *first):
        group, start = place[k]
        return spread(rows, start, attended[group], hidden[group], w_out, first)

    mine1, left1, right1, far1 = block_sums(1)
    far1 = send(far1, LEFT)
    from_left1 = send(right1, RIGHT)
    mine2, left2, right2, far2 = block_sums(2, mine1)
    far2 = send(far2, RIGHT)
    from_right1 = send(added(left1, far1), LEFT)
    from_right2 = send(left2, LEFT)
    from_left2 = send(added(right2, far2), RIGHT)
    mine3, left3, right3, far3 = block_sums(3, mine2, far2, far1)
    up1 = send(added(mine1, from_left1, from_right1), UP)
    far3 = send(far3, LEFT)
    from_left3 = send(right3, RIGHT)
    mine0, left0, right0, far0 = block_sums(0, mine3, far3, up1)
    far0 = send(far0, RIGHT)
    from_right3 = send(added(left3, far3), LEFT)
    up2 = send(added(mine2, from_left2, from_right2, up1), UP)
    from_right0 = send(left0, LEFT)
    from_left0 = send(added(right0, far0), RIGHT)
    up3 = send(added(mine3, from_left3, from_right3, up2), UP)
    return added(tokens, mine0, from_left0, from_right0, up3)


def solution(mesh):
    placed = (
        P(("dp", "mp"), None),
        P(),
        P(None, None, "mp"),
        P(),
        P(),
        P(None, "mp"),
        P("mp"),
        P("mp", None),
        P("mp", None),
    )
    return jax.shard_map(
        shards, mesh=mesh, in_specs=placed, out_specs=P(("dp", "mp"), None), check_vma=False
    )
```

```python
import functools
import math

import jax
import jax.numpy as jnp
from jax import lax
from jax.experimental import pallas as pl
from jax.experimental.pallas import tpu as pltpu
from jax.sharding import PartitionSpec as P

HEAD_DIM = 128
NX = 4
NZ = 4
BF16 = jnp.bfloat16
F32 = jnp.float32
MIB = 1 << 20


Z_NEXT = (1, 3, 0, 2)


def moves(dx, up, dc):
    pairs = []
    for x in range(NX):
        for z in range(NZ):
            for c in range(2):
                to = (((x + dx) % NX) * NZ + (Z_NEXT[z] if up else z)) * 2 + (c + dc) % 2
                pairs.append(((x * NZ + z) * 2 + c, to))
    return pairs


RIGHT = moves(1, False, 0)
LEFT = moves(-1, False, 0)
UP = moves(0, True, 0)
TWIN = moves(0, False, 1)


TWINS = [[2 * i, 2 * i + 1] for i in range(NX * NZ)]


def send(rows, way):
    return lax.ppermute(rows, "mp", way)


def both(array):
    return lax.all_gather(array, "mp", axis_index_groups=TWINS)


def whole(count):
    return [pl.BlockSpec(memory_space=pltpu.VMEM)] * count


CORE = [pl.BlockSpec(memory_space=pltpu.SMEM)]
ANYWHERE = pl.BlockSpec(memory_space=pl.ANY)


def dot(a, b):
    return jnp.dot(a, b, preferred_element_type=F32)


def normalize(rows, gain):
    values = rows.astype(F32)
    mean = jnp.mean(values, axis=-1, keepdims=True)
    centred = values - mean
    spread = jnp.mean(centred * centred, axis=-1, keepdims=True)
    return centred * lax.rsqrt(spread + 1e-06) * gain


def norm_kernel(rows_ref, gain_ref, out_ref):
    out_ref[...] = normalize(rows_ref[...], gain_ref[...].reshape(1, -1)).astype(BF16)


def norm_rows(tokens, gain):
    return pl.pallas_call(
        norm_kernel, out_shape=jax.ShapeDtypeStruct(tokens.shape, BF16)
    )(tokens, gain)


def nothing_kernel(*_):
    pass


def gate(array, *first):
    return pl.pallas_call(
        nothing_kernel,
        in_specs=[pl.BlockSpec(memory_space=pl.ANY)] * (1 + len(first)),
        out_specs=pl.BlockSpec(memory_space=pl.ANY),
        out_shape=jax.ShapeDtypeStruct(array.shape, array.dtype),
        input_output_aliases={0: 0},
        compiler_params=pltpu.CompilerParams(vmem_limit_bytes=MIB),
        cost_estimate=pl.CostEstimate(flops=0, bytes_accessed=0, transcendentals=0),
    )(array, *first)


def project_kernel(count, *refs):
    pieces, rest = refs[:count], refs[count:]
    core, qkv_both, up_own, up_twin, q_gain, k_gain, bias_both = rest[:7]
    query, key_value, hidden, rows = rest[-4:]
    size = pieces[0].shape[0]
    head = HEAD_DIM
    for i, piece in enumerate(pieces):
        rows[pl.ds(i * size, size), :] = piece[...]
    for t, up in enumerate((up_own, up_twin)):
        which = core[0] if t == 0 else 1 - core[0]
        bias = bias_both[which]
        first = dot(rows[...], jnp.concatenate([qkv_both[which, 0], qkv_both[which, 1]], axis=1))
        query[:, t * head : (t + 1) * head] = normalize(
            first[:, :head], q_gain[...].reshape(1, -1)
        ).astype(BF16)
        at = 2 * t * head
        key_value[:, at : at + head] = normalize(
            first[:, head:], k_gain[...].reshape(1, -1)
        ).astype(BF16)
        second = dot(rows[...], jnp.concatenate([qkv_both[which, 2], up[:, :head]], axis=1))
        key_value[:, at + head : at + 2 * head] = second[:, :head].astype(BF16)
        at = 3 * t * head
        hidden[:, at : at + head] = jax.nn.gelu(second[:, head:] + bias[:, :head]).astype(BF16)
        third = dot(rows[...], up[:, head:])
        hidden[:, at + head : at + 3 * head] = jax.nn.gelu(third + bias[:, head:]).astype(BF16)


def project(pieces, weights, first=()):
    size, depth = pieces[0].shape
    count = len(pieces) * size
    return pl.pallas_call(
        functools.partial(project_kernel, len(pieces)),
        in_specs=whole(len(pieces)) + CORE + whole(6) + [ANYWHERE] * len(first),
        out_specs=whole(3),
        out_shape=[jax.ShapeDtypeStruct((count, n * HEAD_DIM), BF16) for n in (2, 4, 6)],
        scratch_shapes=[pltpu.VMEM((count, depth), BF16)],
        compiler_params=pltpu.CompilerParams(vmem_limit_bytes=20 * MIB),
        cost_estimate=pl.CostEstimate(
            flops=24 * count * depth * HEAD_DIM,
            bytes_accessed=24 * depth * HEAD_DIM + 2 * count * depth,
            transcendentals=6 * count * HEAD_DIM,
        ),
    )(*pieces, *weights, *first)


def attend_kernel(count, size, *refs):
    query_refs, own_refs, twin_refs, out_refs = (
        refs[i * count : (i + 1) * count] for i in range(4)
    )

    def image(some, m, at):
        return [
            ref[pl.ds((j * NX + m) * size, size), at : at + HEAD_DIM]
            for ref in some
            for j in range(ref.shape[0] // (NX * size))
        ]

    for m in range(NX):
        for t in range(2):
            own, twin = 2 * t * HEAD_DIM, 2 * (1 - t) * HEAD_DIM
            query = jnp.concatenate(image(query_refs, m, t * HEAD_DIM), axis=0)
            key_rows = jnp.concatenate(image(own_refs, m, own) + image(twin_refs, m, twin), axis=0)
            value = jnp.concatenate(
                image(own_refs, m, own + HEAD_DIM) + image(twin_refs, m, twin + HEAD_DIM), axis=0
            )
            scores = lax.dot_general(
                query, key_rows, (((1,), (1,)), ((), ())), preferred_element_type=F32
            )
            expo = jnp.exp(scores / math.sqrt(HEAD_DIM))
            weights = (expo / jnp.sum(expo, axis=-1, keepdims=True)).astype(BF16)
            mixed = dot(weights, value).astype(BF16)
            at = 0
            for ref in out_refs:
                for j in range(ref.shape[0] // (NX * size)):
                    ref[pl.ds((j * NX + m) * size, size), t * HEAD_DIM : (t + 1) * HEAD_DIM] = mixed[
                        at : at + size
                    ]
                    at += size


def attend(size, query, own, twin):
    return pl.pallas_call(
        functools.partial(attend_kernel, len(query), size),
        in_specs=whole(3 * len(query)),
        out_specs=whole(len(query)),
        out_shape=[jax.ShapeDtypeStruct(a.shape, BF16) for a in query],
        compiler_params=pltpu.CompilerParams(vmem_limit_bytes=12 * MIB),
        cost_estimate=pl.CostEstimate(
            flops=140_000_000, bytes_accessed=2_000_000, transcendentals=270_000
        ),
    )(*query, *own, *twin)


def spread_kernel(start, att, hid, core, attn_both, down_both, *rest):
    outs = rest[-NX:]
    size = outs[0].shape[0]
    own, twin = core[0], 1 - core[0]
    left = jnp.concatenate([att[pl.ds(start, NX * size), :], hid[pl.ds(start, NX * size), :]], axis=1)
    right = jnp.concatenate([attn_both[own], attn_both[twin], down_both[own], down_both[twin]], axis=0)
    partial = dot(left, right).astype(BF16)
    for m, out in enumerate(outs):
        out[...] = partial[m * size : (m + 1) * size]


def spread(size, start, att, hid, weights, first):
    depth = weights[1].shape[2]
    return pl.pallas_call(
        functools.partial(spread_kernel, start),
        in_specs=whole(2) + CORE + whole(2) + [pl.BlockSpec(memory_space=pl.ANY)] * len(first),
        out_specs=whole(NX),
        out_shape=[jax.ShapeDtypeStruct((size, depth), BF16)] * NX,
        compiler_params=pltpu.CompilerParams(vmem_limit_bytes=16 * MIB),
        cost_estimate=pl.CostEstimate(
            flops=16 * NX * size * depth * HEAD_DIM,
            bytes_accessed=16 * depth * HEAD_DIM + 2 * NX * size * depth,
            transcendentals=0,
        ),
    )(att, hid, *weights, *first)


def added(*parts):
    return sum(p.astype(F32) for p in parts).astype(BF16)


def shards(tokens, ln_gain, w_qkv, q_gain, k_gain, w_up, up_bias, w_out_attn, w_down):
    rows, depth = tokens.shape
    core = (lax.axis_index("mp") % 2).reshape(1)
    bias_both = both(up_bias.reshape(1, -1))
    qkv_both = both(jnp.transpose(w_qkv, (1, 0, 2)))
    w_in = (core, qkv_both, w_up, send(w_up, TWIN), q_gain, k_gain, bias_both)
    w_out = (core, both(w_out_attn), both(w_down))

    held, left, right, far = {}, {}, {}, {}
    held[0] = norm_rows(tokens, ln_gain)
    next1 = send(held[0], UP)
    left[0] = send(held[0], RIGHT)
    right[0] = send(held[0], LEFT)
    held[1] = gate(next1, left[0], right[0], w_in[3])
    next2 = send(held[1], UP)
    far[0] = send(left[0], RIGHT)
    right[1] = send(held[1], LEFT)
    left[1] = send(held[1], RIGHT)
    far[1] = send(right[1], LEFT)
    held[2] = gate(next2, far[0], right[1], left[1])
    next3 = send(held[2], UP)
    left[2] = send(held[2], RIGHT)
    right[2] = send(held[2], LEFT)
    far[2] = send(left[2], RIGHT)
    held[3] = gate(next3, far[1], left[2], right[2], w_in[1])
    right[3] = send(held[3], LEFT)
    left[3] = send(held[3], RIGHT)
    far[3] = send(right[3], LEFT)
    pieces = [[held[k], left[k], right[k], far[k]] for k in range(NZ)]

    groups = [pieces[0] + pieces[1], pieces[2], pieces[3]]
    query, own, hidden = zip(
        project(groups[0], w_in), project(groups[1], w_in, w_out[1:]), project(groups[2], w_in)
    )
    twin = [send(part, TWIN) for part in own]
    attended = attend(rows, query, own, twin)

    block_rows = NX * rows
    place = {0: (0, 0), 1: (0, block_rows), 2: (1, 0), 3: (2, 0)}

    def block_sums(k, *first):
        group, start = place[k]
        return spread(rows, start, attended[group], hidden[group], w_out, first)

    mine1, left1, right1, far1 = block_sums(1)
    far1 = send(far1, LEFT)
    from_left1 = send(right1, RIGHT)
    mine2, left2, right2, far2 = block_sums(2, mine1)
    far2 = send(far2, RIGHT)
    from_right1 = send(added(left1, far1), LEFT)
    from_right2 = send(left2, LEFT)
    from_left2 = send(added(right2, far2), RIGHT)
    mine3, left3, right3, far3 = block_sums(3, mine2, far2, far1)
    up1 = send(added(mine1, from_left1, from_right1), UP)
    far3 = send(far3, LEFT)
    from_left3 = send(right3, RIGHT)
    mine0, left0, right0, far0 = block_sums(0, mine3, far3, up1)
    far0 = send(far0, RIGHT)
    from_right3 = send(added(left3, far3), LEFT)
    up2 = send(added(mine2, from_left2, from_right2, up1), UP)
    from_right0 = send(left0, LEFT)
    from_left0 = send(added(right0, far0), RIGHT)
    up3 = send(added(mine3, from_left3, from_right3, up2), UP)
    return added(tokens, mine0, from_left0, from_right0, up3)


def solution(mesh):
    placed = (
        P(("dp", "mp"), None),
        P(),
        P(None, None, "mp"),
        P(),
        P(),
        P(None, "mp"),
        P("mp"),
        P("mp", None),
        P("mp", None),
    )
    return jax.shard_map(
        shards, mesh=mesh, in_specs=placed, out_specs=P(("dp", "mp"), None), check_vma=False
    )
```

```python
import functools
import math

import jax
import jax.numpy as jnp
from jax import lax
from jax.experimental import pallas as pl
from jax.experimental.pallas import tpu as pltpu
from jax.sharding import PartitionSpec as P

HEAD_DIM = 128
NX = 4
NZ = 4
BF16 = jnp.bfloat16
F32 = jnp.float32
MIB = 1 << 20


Z_NEXT = (1, 3, 0, 2)


def moves(dx, up, dc):
    pairs = []
    for x in range(NX):
        for z in range(NZ):
            for c in range(2):
                to = (((x + dx) % NX) * NZ + (Z_NEXT[z] if up else z)) * 2 + (c + dc) % 2
                pairs.append(((x * NZ + z) * 2 + c, to))
    return pairs


RIGHT = moves(1, False, 0)
LEFT = moves(-1, False, 0)
UP = moves(0, True, 0)
TWIN = moves(0, False, 1)


def send(rows, way):
    return lax.ppermute(rows, "mp", way)


def whole(count):
    return [pl.BlockSpec(memory_space=pltpu.VMEM)] * count


def dot(a, b):
    return jnp.dot(a, b, preferred_element_type=F32)


def normalize(rows, gain):
    values = rows.astype(F32)
    mean = jnp.mean(values, axis=-1, keepdims=True)
    centred = values - mean
    spread = jnp.mean(centred * centred, axis=-1, keepdims=True)
    return centred * lax.rsqrt(spread + 1e-06) * gain


def norm_kernel(rows_ref, gain_ref, out_ref):
    out_ref[...] = normalize(rows_ref[...], gain_ref[...].reshape(1, -1)).astype(BF16)


def norm_rows(tokens, gain):
    return pl.pallas_call(
        norm_kernel, out_shape=jax.ShapeDtypeStruct(tokens.shape, BF16)
    )(tokens, gain)


def pack_kernel(skipped, *refs):
    parts, out = refs[skipped:-1], refs[-1]
    at = 0
    for part in parts:
        out[pl.ds(at, part.shape[0])] = part[...]
        at += part.shape[0]


def pack(shape, first, *parts):
    return pl.pallas_call(
        functools.partial(pack_kernel, len(first)),
        in_specs=[pl.BlockSpec(memory_space=pl.ANY)] * len(first) + whole(len(parts)),
        out_specs=pl.BlockSpec(memory_space=pltpu.VMEM),
        out_shape=jax.ShapeDtypeStruct(shape, parts[0].dtype),
        compiler_params=pltpu.CompilerParams(vmem_limit_bytes=20 * MIB),
        cost_estimate=pl.CostEstimate(
            flops=0, bytes_accessed=sum(4 * a.size for a in parts), transcendentals=0
        ),
    )(*first, *parts)


def nothing_kernel(*_):
    pass


def gate(array, *first):
    return pl.pallas_call(
        nothing_kernel,
        in_specs=[pl.BlockSpec(memory_space=pl.ANY)] * (1 + len(first)),
        out_specs=pl.BlockSpec(memory_space=pl.ANY),
        out_shape=jax.ShapeDtypeStruct(array.shape, array.dtype),
        input_output_aliases={0: 0},
        compiler_params=pltpu.CompilerParams(vmem_limit_bytes=MIB),
        cost_estimate=pl.CostEstimate(flops=0, bytes_accessed=0, transcendentals=0),
    )(array, *first)


def project_kernel(count, *refs):
    pieces, rest = refs[:count], refs[count:]
    qkv_own, qkv_twin, up_own, up_twin, q_gain, k_gain, bias_own, bias_twin = rest[:8]
    query, key_value, hidden, rows = rest[8:]
    size = pieces[0].shape[0]
    head = HEAD_DIM
    for i, piece in enumerate(pieces):
        rows[pl.ds(i * size, size), :] = piece[...]
    for t, (qkv, up, bias_ref) in enumerate(
        ((qkv_own, up_own, bias_own), (qkv_twin, up_twin, bias_twin))
    ):
        bias = bias_ref[...].reshape(1, -1)
        first = dot(rows[...], jnp.concatenate([qkv[0], qkv[1]], axis=1))
        query[:, t * head : (t + 1) * head] = normalize(
            first[:, :head], q_gain[...].reshape(1, -1)
        ).astype(BF16)
        at = 2 * t * head
        key_value[:, at : at + head] = normalize(
            first[:, head:], k_gain[...].reshape(1, -1)
        ).astype(BF16)
        second = dot(rows[...], jnp.concatenate([qkv[2], up[:, :head]], axis=1))
        key_value[:, at + head : at + 2 * head] = second[:, :head].astype(BF16)
        at = 3 * t * head
        hidden[:, at : at + head] = jax.nn.gelu(second[:, head:] + bias[:, :head]).astype(BF16)
        third = dot(rows[...], up[:, head:])
        hidden[:, at + head : at + 3 * head] = jax.nn.gelu(third + bias[:, head:]).astype(BF16)


def project(pieces, *weights):
    size, depth = pieces[0].shape
    count = len(pieces) * size
    return pl.pallas_call(
        functools.partial(project_kernel, len(pieces)),
        in_specs=whole(len(pieces) + 8),
        out_specs=whole(3),
        out_shape=[jax.ShapeDtypeStruct((count, n * HEAD_DIM), BF16) for n in (2, 4, 6)],
        scratch_shapes=[pltpu.VMEM((count, depth), BF16)],
        compiler_params=pltpu.CompilerParams(vmem_limit_bytes=20 * MIB),
        cost_estimate=pl.CostEstimate(
            flops=24 * count * depth * HEAD_DIM,
            bytes_accessed=24 * depth * HEAD_DIM + 2 * count * depth,
            transcendentals=6 * count * HEAD_DIM,
        ),
    )(*pieces, *weights)


def attend_kernel(count, size, *refs):
    query_refs, own_refs, twin_refs, out_refs = (
        refs[i * count : (i + 1) * count] for i in range(4)
    )

    def image(some, m, at):
        return [
            ref[pl.ds((j * NX + m) * size, size), at : at + HEAD_DIM]
            for ref in some
            for j in range(ref.shape[0] // (NX * size))
        ]

    for m in range(NX):
        for t in range(2):
            own, twin = 2 * t * HEAD_DIM, 2 * (1 - t) * HEAD_DIM
            query = jnp.concatenate(image(query_refs, m, t * HEAD_DIM), axis=0)
            key_rows = jnp.concatenate(image(own_refs, m, own) + image(twin_refs, m, twin), axis=0)
            value = jnp.concatenate(
                image(own_refs, m, own + HEAD_DIM) + image(twin_refs, m, twin + HEAD_DIM), axis=0
            )
            scores = lax.dot_general(
                query, key_rows, (((1,), (1,)), ((), ())), preferred_element_type=F32
            )
            expo = jnp.exp(scores / math.sqrt(HEAD_DIM))
            weights = (expo / jnp.sum(expo, axis=-1, keepdims=True)).astype(BF16)
            mixed = dot(weights, value).astype(BF16)
            at = 0
            for ref in out_refs:
                for j in range(ref.shape[0] // (NX * size)):
                    ref[pl.ds((j * NX + m) * size, size), t * HEAD_DIM : (t + 1) * HEAD_DIM] = mixed[
                        at : at + size
                    ]
                    at += size


def attend(size, query, own, twin):
    return pl.pallas_call(
        functools.partial(attend_kernel, len(query), size),
        in_specs=whole(3 * len(query)),
        out_specs=whole(len(query)),
        out_shape=[jax.ShapeDtypeStruct(a.shape, BF16) for a in query],
        compiler_params=pltpu.CompilerParams(vmem_limit_bytes=12 * MIB),
        cost_estimate=pl.CostEstimate(
            flops=140_000_000, bytes_accessed=2_000_000, transcendentals=270_000
        ),
    )(*query, *own, *twin)


def spread_kernel(start, att, hid, out_own, out_twin, *rest):
    outs = rest[-NX:]
    size = outs[0].shape[0]
    head = HEAD_DIM
    span = pl.ds(start, NX * size)
    left = jnp.concatenate(
        [att[span, :head], hid[span, : 3 * head], att[span, head:], hid[span, 3 * head :]], axis=1
    )
    right = jnp.concatenate([out_own[...], out_twin[...]], axis=0)
    partial = dot(left, right).astype(BF16)
    for m, out in enumerate(outs):
        out[...] = partial[m * size : (m + 1) * size]


def spread(size, start, att, hid, weights, first):
    depth = weights[0].shape[1]
    return pl.pallas_call(
        functools.partial(spread_kernel, start),
        in_specs=whole(4) + [pl.BlockSpec(memory_space=pl.ANY)] * len(first),
        out_specs=whole(NX),
        out_shape=[jax.ShapeDtypeStruct((size, depth), BF16)] * NX,
        compiler_params=pltpu.CompilerParams(vmem_limit_bytes=16 * MIB),
        cost_estimate=pl.CostEstimate(
            flops=16 * NX * size * depth * HEAD_DIM,
            bytes_accessed=16 * depth * HEAD_DIM + 2 * NX * size * depth,
            transcendentals=0,
        ),
    )(att, hid, *weights, *first)


def added(*parts):
    return sum(p.astype(F32) for p in parts).astype(BF16)


def shards(tokens, ln_gain, w_qkv, q_gain, k_gain, w_up, up_bias, w_out_attn, w_down):
    rows, depth = tokens.shape
    w_qkv = jnp.transpose(w_qkv, (1, 0, 2))
    up_twin, qkv_twin = send(w_up, TWIN), send(w_qkv, TWIN)

    held, left, right, far = {}, {}, {}, {}
    held[0] = norm_rows(tokens, ln_gain)
    next1 = send(held[0], UP)
    left[0] = send(held[0], RIGHT)
    right[0] = send(held[0], LEFT)
    held[1] = gate(next1, left[0], right[0], up_twin, qkv_twin)
    next2 = send(held[1], UP)
    far[0] = send(left[0], RIGHT)
    right[1] = send(held[1], LEFT)
    left[1] = send(held[1], RIGHT)
    far[1] = send(right[1], LEFT)
    held[2] = gate(next2, far[0], right[1])
    next3 = send(held[2], UP)
    left[2] = send(held[2], RIGHT)
    right[2] = send(held[2], LEFT)
    far[2] = send(left[2], RIGHT)
    held[3] = gate(next3, far[1], left[1], left[2], right[2])
    right[3] = send(held[3], LEFT)
    left[3] = send(held[3], RIGHT)
    far[3] = send(right[3], LEFT)
    pieces = [[held[k], left[k], right[k], far[k]] for k in range(NZ)]

    bias_twin = send(pack(up_bias.shape, (left[1],), up_bias), TWIN)
    out_own = pack(
        (4 * HEAD_DIM, depth), (far[1], left[2], right[2], next3, bias_twin), w_out_attn, w_down
    )
    w_in = (w_qkv, qkv_twin, w_up, up_twin, q_gain, k_gain, up_bias, bias_twin)
    w_out = (out_own, send(out_own, TWIN))

    groups = [pieces[0] + pieces[1], pieces[2], pieces[3]]
    query, own, hidden = zip(*[project(group, *w_in) for group in groups])
    twin = [send(part, TWIN) for part in own]
    attended = attend(rows, query, own, twin)

    block_rows = NX * rows
    place = {0: (0, 0), 1: (0, block_rows), 2: (1, 0), 3: (2, 0)}

    def block_sums(k, *first):
        group, start = place[k]
        return spread(rows, start, attended[group], hidden[group], w_out, first)

    mine1, left1, right1, far1 = block_sums(1)
    far1 = send(far1, LEFT)
    from_left1 = send(right1, RIGHT)
    mine2, left2, right2, far2 = block_sums(2, mine1)
    far2 = send(far2, RIGHT)
    from_right1 = send(added(left1, far1), LEFT)
    from_right2 = send(left2, LEFT)
    from_left2 = send(added(right2, far2), RIGHT)
    mine3, left3, right3, far3 = block_sums(3, mine2, far2, far1)
    up1 = send(added(mine1, from_left1, from_right1), UP)
    far3 = send(far3, LEFT)
    from_left3 = send(right3, RIGHT)
    mine0, left0, right0, far0 = block_sums(0, mine3, far3, up1)
    far0 = send(far0, RIGHT)
    from_right3 = send(added(left3, far3), LEFT)
    up2 = send(added(mine2, from_left2, from_right2, up1), UP)
    from_right0 = send(left0, LEFT)
    from_left0 = send(added(right0, far0), RIGHT)
    up3 = send(added(mine3, from_left3, from_right3, up2), UP)
    return added(tokens, mine0, from_left0, from_right0, up3)


def solution(mesh):
    placed = (
        P(("dp", "mp"), None),
        P(),
        P(None, None, "mp"),
        P(),
        P(),
        P(None, "mp"),
        P("mp"),
        P("mp", None),
        P("mp", None),
    )
    return jax.shard_map(
        shards, mesh=mesh, in_specs=placed, out_specs=P(("dp", "mp"), None), check_vma=False
    )
```

```python
import functools
import math

import jax
import jax.numpy as jnp
from jax import lax
from jax.experimental import pallas as pl
from jax.experimental.pallas import tpu as pltpu
from jax.sharding import PartitionSpec as P

HEAD_DIM = 128
NX = 4
NZ = 4
BF16 = jnp.bfloat16
F32 = jnp.float32
MIB = 1 << 20


Z_NEXT = (1, 3, 0, 2)


def moves(dx, up, dc):
    pairs = []
    for x in range(NX):
        for z in range(NZ):
            for c in range(2):
                to = (((x + dx) % NX) * NZ + (Z_NEXT[z] if up else z)) * 2 + (c + dc) % 2
                pairs.append(((x * NZ + z) * 2 + c, to))
    return pairs


RIGHT = moves(1, False, 0)
LEFT = moves(-1, False, 0)
UP = moves(0, True, 0)
TWIN = moves(0, False, 1)


def send(rows, way):
    return lax.ppermute(rows, "mp", way)


def whole(count):
    return [pl.BlockSpec(memory_space=pltpu.VMEM)] * count


def dot(a, b):
    return jnp.dot(a, b, preferred_element_type=F32)


def normalize(rows, gain):
    values = rows.astype(F32)
    mean = jnp.mean(values, axis=-1, keepdims=True)
    centred = values - mean
    spread = jnp.mean(centred * centred, axis=-1, keepdims=True)
    return centred * lax.rsqrt(spread + 1e-06) * gain


def norm_kernel(rows_ref, gain_ref, out_ref):
    out_ref[...] = normalize(rows_ref[...], gain_ref[...].reshape(1, -1)).astype(BF16)


def norm_rows(tokens, gain):
    return pl.pallas_call(
        norm_kernel, out_shape=jax.ShapeDtypeStruct(tokens.shape, BF16)
    )(tokens, gain)


def pack_kernel(skipped, *refs):
    parts, out = refs[skipped:-1], refs[-1]
    at = 0
    for part in parts:
        out[pl.ds(at, part.shape[0])] = part[...]
        at += part.shape[0]


def pack(shape, first, *parts):
    return pl.pallas_call(
        functools.partial(pack_kernel, len(first)),
        in_specs=[pl.BlockSpec(memory_space=pl.ANY)] * len(first) + whole(len(parts)),
        out_specs=pl.BlockSpec(memory_space=pltpu.VMEM),
        out_shape=jax.ShapeDtypeStruct(shape, parts[0].dtype),
        compiler_params=pltpu.CompilerParams(vmem_limit_bytes=11 * MIB),
        cost_estimate=pl.CostEstimate(
            flops=0, bytes_accessed=sum(4 * a.size for a in parts), transcendentals=0
        ),
    )(*first, *parts)


def nothing_kernel(*_):
    pass


def gate(array, *first):
    return pl.pallas_call(
        nothing_kernel,
        in_specs=[pl.BlockSpec(memory_space=pl.ANY)] * (1 + len(first)),
        out_specs=pl.BlockSpec(memory_space=pl.ANY),
        out_shape=jax.ShapeDtypeStruct(array.shape, array.dtype),
        input_output_aliases={0: 0},
        compiler_params=pltpu.CompilerParams(vmem_limit_bytes=MIB),
        cost_estimate=pl.CostEstimate(flops=0, bytes_accessed=0, transcendentals=0),
    )(array, *first)


def project_kernel(count, keep, *refs):
    pieces, rest = refs[:count], refs[count:]
    qkv_own, qkv_twin, up_own, up_twin, q_gain, k_gain, bias_own, bias_twin = rest[:8]
    query, key_value, hidden, *kept, rows = rest[8:]
    if keep:
        kept[0][...] = qkv_twin[...]
    size = pieces[0].shape[0]
    head = HEAD_DIM
    for i, piece in enumerate(pieces):
        rows[pl.ds(i * size, size), :] = piece[...]
    for t, (qkv, up, bias_ref) in enumerate(
        ((qkv_own, up_own, bias_own), (qkv_twin, up_twin, bias_twin))
    ):
        bias = bias_ref[...].reshape(1, -1)
        first = dot(rows[...], jnp.concatenate([qkv[0], qkv[1]], axis=1))
        query[:, t * head : (t + 1) * head] = normalize(
            first[:, :head], q_gain[...].reshape(1, -1)
        ).astype(BF16)
        at = 2 * t * head
        key_value[:, at : at + head] = normalize(
            first[:, head:], k_gain[...].reshape(1, -1)
        ).astype(BF16)
        second = dot(rows[...], jnp.concatenate([qkv[2], up[:, :head]], axis=1))
        key_value[:, at + head : at + 2 * head] = second[:, :head].astype(BF16)
        at = 3 * t * head
        hidden[:, at : at + head] = jax.nn.gelu(second[:, head:] + bias[:, :head]).astype(BF16)
        third = dot(rows[...], up[:, head:])
        hidden[:, at + head : at + 3 * head] = jax.nn.gelu(third + bias[:, head:]).astype(BF16)


def project(pieces, weights, keep=False):
    size, depth = pieces[0].shape
    count = len(pieces) * size
    return pl.pallas_call(
        functools.partial(project_kernel, len(pieces), keep),
        in_specs=whole(len(pieces) + 8),
        out_specs=whole(3 + keep),
        out_shape=[jax.ShapeDtypeStruct((count, n * HEAD_DIM), BF16) for n in (2, 4, 6)]
        + [jax.ShapeDtypeStruct(weights[1].shape, BF16)] * keep,
        scratch_shapes=[pltpu.VMEM((count, depth), BF16)],
        compiler_params=pltpu.CompilerParams(vmem_limit_bytes=24 * MIB),
        cost_estimate=pl.CostEstimate(
            flops=24 * count * depth * HEAD_DIM,
            bytes_accessed=24 * depth * HEAD_DIM + 2 * count * depth,
            transcendentals=6 * count * HEAD_DIM,
        ),
    )(*pieces, *weights)


def attend_kernel(count, size, *refs):
    query_refs, own_refs, twin_refs, out_refs = (
        refs[i * count : (i + 1) * count] for i in range(4)
    )

    def image(some, m, at):
        return [
            ref[pl.ds((j * NX + m) * size, size), at : at + HEAD_DIM]
            for ref in some
            for j in range(ref.shape[0] // (NX * size))
        ]

    for m in range(NX):
        for t in range(2):
            own, twin = 2 * t * HEAD_DIM, 2 * (1 - t) * HEAD_DIM
            query = jnp.concatenate(image(query_refs, m, t * HEAD_DIM), axis=0)
            key_rows = jnp.concatenate(image(own_refs, m, own) + image(twin_refs, m, twin), axis=0)
            value = jnp.concatenate(
                image(own_refs, m, own + HEAD_DIM) + image(twin_refs, m, twin + HEAD_DIM), axis=0
            )
            scores = lax.dot_general(
                query, key_rows, (((1,), (1,)), ((), ())), preferred_element_type=F32
            )
            expo = jnp.exp(scores / math.sqrt(HEAD_DIM))
            weights = (expo / jnp.sum(expo, axis=-1, keepdims=True)).astype(BF16)
            mixed = dot(weights, value).astype(BF16)
            at = 0
            for ref in out_refs:
                for j in range(ref.shape[0] // (NX * size)):
                    ref[pl.ds((j * NX + m) * size, size), t * HEAD_DIM : (t + 1) * HEAD_DIM] = mixed[
                        at : at + size
                    ]
                    at += size


def attend(size, query, own, twin):
    return pl.pallas_call(
        functools.partial(attend_kernel, len(query), size),
        in_specs=whole(3 * len(query)),
        out_specs=whole(len(query)),
        out_shape=[jax.ShapeDtypeStruct(a.shape, BF16) for a in query],
        compiler_params=pltpu.CompilerParams(vmem_limit_bytes=12 * MIB),
        cost_estimate=pl.CostEstimate(
            flops=140_000_000, bytes_accessed=2_000_000, transcendentals=270_000
        ),
    )(*query, *own, *twin)


def spread_kernel(start, att, hid, out_own, out_twin, *rest):
    outs = rest[-NX:]
    size = outs[0].shape[0]
    head = HEAD_DIM
    span = pl.ds(start, NX * size)
    left = jnp.concatenate(
        [att[span, :head], hid[span, : 3 * head], att[span, head:], hid[span, 3 * head :]], axis=1
    )
    right = jnp.concatenate([out_own[...], out_twin[...]], axis=0)
    partial = dot(left, right).astype(BF16)
    for m, out in enumerate(outs):
        out[...] = partial[m * size : (m + 1) * size]


def spread(size, start, att, hid, weights, first):
    depth = weights[0].shape[1]
    return pl.pallas_call(
        functools.partial(spread_kernel, start),
        in_specs=whole(4) + [pl.BlockSpec(memory_space=pl.ANY)] * len(first),
        out_specs=whole(NX),
        out_shape=[jax.ShapeDtypeStruct((size, depth), BF16)] * NX,
        compiler_params=pltpu.CompilerParams(vmem_limit_bytes=16 * MIB),
        cost_estimate=pl.CostEstimate(
            flops=16 * NX * size * depth * HEAD_DIM,
            bytes_accessed=16 * depth * HEAD_DIM + 2 * NX * size * depth,
            transcendentals=0,
        ),
    )(att, hid, *weights, *first)


def added(*parts):
    return sum(p.astype(F32) for p in parts).astype(BF16)


def shards(tokens, ln_gain, w_qkv, q_gain, k_gain, w_up, up_bias, w_out_attn, w_down):
    rows, depth = tokens.shape
    w_qkv = jnp.transpose(w_qkv, (1, 0, 2))
    up_twin, qkv_twin = send(w_up, TWIN), send(w_qkv, TWIN)

    held, left, right, far = {}, {}, {}, {}
    held[0] = norm_rows(tokens, ln_gain)
    next1 = send(held[0], UP)
    left[0] = send(held[0], RIGHT)
    right[0] = send(held[0], LEFT)
    held[1] = gate(next1, left[0], right[0], up_twin, qkv_twin)
    next2 = send(held[1], UP)
    far[0] = send(left[0], RIGHT)
    right[1] = send(held[1], LEFT)
    left[1] = send(held[1], RIGHT)
    far[1] = send(right[1], LEFT)
    held[2] = gate(next2, far[0], right[1])
    next3 = send(held[2], UP)
    left[2] = send(held[2], RIGHT)
    right[2] = send(held[2], LEFT)
    far[2] = send(left[2], RIGHT)
    held[3] = gate(next3, far[1], left[1], left[2], right[2])
    right[3] = send(held[3], LEFT)
    left[3] = send(held[3], RIGHT)
    bias_twin = send(pack(up_bias.shape, (left[1],), up_bias), TWIN)
    out_own = pack(
        (4 * HEAD_DIM, depth), (far[1], left[2], right[2], next3, bias_twin), w_out_attn, w_down
    )
    w_in = (w_qkv, qkv_twin, w_up, up_twin, q_gain, k_gain, up_bias, bias_twin)
    w_out = (out_own, send(out_own, TWIN))

    def rows_of(*blocks):
        return [a[k] for k in blocks for a in (held, left, right, far)]

    *early, kept = project(rows_of(0, 1), w_in, keep=True)
    far[3] = send(gate(right[3], early[0]), LEFT)
    w_in = (w_qkv, kept, *w_in[2:])
    query, own, hidden = zip(early, project(rows_of(2), w_in), project(rows_of(3), w_in))
    twin = [send(part, TWIN) for part in own]
    attended = attend(rows, query, own, twin)

    block_rows = NX * rows
    place = {0: (0, 0), 1: (0, block_rows), 2: (1, 0), 3: (2, 0)}

    def block_sums(k, *first):
        group, start = place[k]
        return spread(rows, start, attended[group], hidden[group], w_out, first)

    mine1, left1, right1, far1 = block_sums(1)
    far1 = send(far1, LEFT)
    from_left1 = send(right1, RIGHT)
    mine2, left2, right2, far2 = block_sums(2, mine1)
    far2 = send(far2, RIGHT)
    from_right1 = send(added(left1, far1), LEFT)
    from_right2 = send(left2, LEFT)
    from_left2 = send(added(right2, far2), RIGHT)
    mine3, left3, right3, far3 = block_sums(3, mine2, far2, far1)
    sum1 = added(mine1, from_left1, from_right1)
    up1 = send(sum1, UP)
    far3 = send(far3, LEFT)
    from_left3 = send(right3, RIGHT)
    mine0, left0, right0, far0 = block_sums(0, mine3, sum1)
    far0 = send(far0, RIGHT)
    from_right3 = send(added(left3, far3), LEFT)
    up2 = send(added(mine2, from_left2, from_right2, up1), UP)
    from_right0 = send(gate(left0, up1), LEFT)
    from_left0 = send(added(right0, far0), RIGHT)
    up3 = send(added(mine3, from_left3, from_right3, up2), UP)
    return added(tokens, mine0, from_left0, from_right0, up3)


def solution(mesh):
    placed = (
        P(("dp", "mp"), None),
        P(),
        P(None, None, "mp"),
        P(),
        P(),
        P(None, "mp"),
        P("mp"),
        P("mp", None),
        P("mp", None),
    )
    return jax.shard_map(
        shards, mesh=mesh, in_specs=placed, out_specs=P(("dp", "mp"), None), check_vma=False
    )
```

```python
import functools
import math

import jax
import jax.numpy as jnp
from jax import lax
from jax.experimental import pallas as pl
from jax.experimental.pallas import tpu as pltpu
from jax.sharding import PartitionSpec as P

HEAD_DIM = 128
NX = 4
NZ = 4
BF16 = jnp.bfloat16
F32 = jnp.float32
MIB = 1 << 20


Z_NEXT = (1, 3, 0, 2)


def moves(dx, up, dc):
    pairs = []
    for x in range(NX):
        for z in range(NZ):
            for c in range(2):
                to = (((x + dx) % NX) * NZ + (Z_NEXT[z] if up else z)) * 2 + (c + dc) % 2
                pairs.append(((x * NZ + z) * 2 + c, to))
    return pairs


RIGHT = moves(1, False, 0)
LEFT = moves(-1, False, 0)
UP = moves(0, True, 0)
TWIN = moves(0, False, 1)


def send(rows, way):
    return lax.ppermute(rows, "mp", way)


def whole(count):
    return [pl.BlockSpec(memory_space=pltpu.VMEM)] * count


def dot(a, b):
    return jnp.dot(a, b, preferred_element_type=F32)


def normalize(rows, gain):
    values = rows.astype(F32)
    mean = jnp.mean(values, axis=-1, keepdims=True)
    centred = values - mean
    spread = jnp.mean(centred * centred, axis=-1, keepdims=True)
    return centred * lax.rsqrt(spread + 1e-06) * gain


def norm_kernel(rows_ref, gain_ref, out_ref):
    out_ref[...] = normalize(rows_ref[...], gain_ref[...].reshape(1, -1)).astype(BF16)


def norm_rows(tokens, gain):
    return pl.pallas_call(
        norm_kernel, out_shape=jax.ShapeDtypeStruct(tokens.shape, BF16)
    )(tokens, gain)


def pack_kernel(skipped, *refs):
    parts, out = refs[skipped:-1], refs[-1]
    at = 0
    for part in parts:
        out[pl.ds(at, part.shape[0])] = part[...]
        at += part.shape[0]


def pack(shape, first, *parts):
    return pl.pallas_call(
        functools.partial(pack_kernel, len(first)),
        in_specs=[pl.BlockSpec(memory_space=pl.ANY)] * len(first) + whole(len(parts)),
        out_specs=pl.BlockSpec(memory_space=pltpu.VMEM),
        out_shape=jax.ShapeDtypeStruct(shape, parts[0].dtype),
        compiler_params=pltpu.CompilerParams(vmem_limit_bytes=11 * MIB),
        cost_estimate=pl.CostEstimate(
            flops=0, bytes_accessed=sum(4 * a.size for a in parts), transcendentals=0
        ),
    )(*first, *parts)


def nothing_kernel(*_):
    pass


def gate(array, *first):
    return pl.pallas_call(
        nothing_kernel,
        in_specs=[pl.BlockSpec(memory_space=pl.ANY)] * (1 + len(first)),
        out_specs=pl.BlockSpec(memory_space=pl.ANY),
        out_shape=jax.ShapeDtypeStruct(array.shape, array.dtype),
        input_output_aliases={0: 0},
        compiler_params=pltpu.CompilerParams(vmem_limit_bytes=MIB),
        cost_estimate=pl.CostEstimate(flops=0, bytes_accessed=0, transcendentals=0),
    )(array, *first)


def project_kernel(count, keep, *refs):
    pieces, rest = refs[:count], refs[count:]
    qkv_own, qkv_twin, up_own, up_twin, q_gain, k_gain, bias_own, bias_twin = rest[:8]
    query, key_value, hidden, *kept, rows = rest[8:]
    if keep:
        kept[0][...] = qkv_twin[...]
    size = pieces[0].shape[0]
    head = HEAD_DIM
    for i, piece in enumerate(pieces):
        rows[pl.ds(i * size, size), :] = piece[...]
    for t, (qkv, up, bias_ref) in enumerate(
        ((qkv_own, up_own, bias_own), (qkv_twin, up_twin, bias_twin))
    ):
        bias = bias_ref[...].reshape(1, -1)
        first = dot(rows[...], jnp.concatenate([qkv[0], qkv[1]], axis=1))
        query[:, t * head : (t + 1) * head] = normalize(
            first[:, :head], q_gain[...].reshape(1, -1)
        ).astype(BF16)
        at = 2 * t * head
        key_value[:, at : at + head] = normalize(
            first[:, head:], k_gain[...].reshape(1, -1)
        ).astype(BF16)
        second = dot(rows[...], jnp.concatenate([qkv[2], up[:, :head]], axis=1))
        key_value[:, at + head : at + 2 * head] = second[:, :head].astype(BF16)
        at = 3 * t * head
        hidden[:, at : at + head] = jax.nn.gelu(second[:, head:] + bias[:, :head]).astype(BF16)
        third = dot(rows[...], up[:, head:])
        hidden[:, at + head : at + 3 * head] = jax.nn.gelu(third + bias[:, head:]).astype(BF16)


def project(pieces, weights, keep=False):
    size, depth = pieces[0].shape
    count = len(pieces) * size
    return pl.pallas_call(
        functools.partial(project_kernel, len(pieces), keep),
        in_specs=whole(len(pieces) + 8),
        out_specs=whole(3 + keep),
        out_shape=[jax.ShapeDtypeStruct((count, n * HEAD_DIM), BF16) for n in (2, 4, 6)]
        + [jax.ShapeDtypeStruct(weights[1].shape, BF16)] * keep,
        scratch_shapes=[pltpu.VMEM((count, depth), BF16)],
        compiler_params=pltpu.CompilerParams(vmem_limit_bytes=24 * MIB),
        cost_estimate=pl.CostEstimate(
            flops=24 * count * depth * HEAD_DIM,
            bytes_accessed=24 * depth * HEAD_DIM + 2 * count * depth,
            transcendentals=6 * count * HEAD_DIM,
        ),
    )(*pieces, *weights)


def attend_kernel(count, size, *refs):
    query_refs, own_refs, twin_refs, out_refs = (
        refs[i * count : (i + 1) * count] for i in range(4)
    )

    def image(some, m, at):
        return [
            ref[pl.ds((j * NX + m) * size, size), at : at + HEAD_DIM]
            for ref in some
            for j in range(ref.shape[0] // (NX * size))
        ]

    for m in range(NX):
        for t in range(2):
            own, twin = 2 * t * HEAD_DIM, 2 * (1 - t) * HEAD_DIM
            query = jnp.concatenate(image(query_refs, m, t * HEAD_DIM), axis=0)
            key_rows = jnp.concatenate(image(own_refs, m, own) + image(twin_refs, m, twin), axis=0)
            value = jnp.concatenate(
                image(own_refs, m, own + HEAD_DIM) + image(twin_refs, m, twin + HEAD_DIM), axis=0
            )
            scores = lax.dot_general(
                query, key_rows, (((1,), (1,)), ((), ())), preferred_element_type=F32
            )
            expo = jnp.exp(scores / math.sqrt(HEAD_DIM))
            weights = (expo / jnp.sum(expo, axis=-1, keepdims=True)).astype(BF16)
            mixed = dot(weights, value).astype(BF16)
            at = 0
            for ref in out_refs:
                for j in range(ref.shape[0] // (NX * size)):
                    ref[pl.ds((j * NX + m) * size, size), t * HEAD_DIM : (t + 1) * HEAD_DIM] = mixed[
                        at : at + size
                    ]
                    at += size


def attend(size, query, own, twin):
    return pl.pallas_call(
        functools.partial(attend_kernel, len(query), size),
        in_specs=whole(3 * len(query)),
        out_specs=whole(len(query)),
        out_shape=[jax.ShapeDtypeStruct(a.shape, BF16) for a in query],
        compiler_params=pltpu.CompilerParams(vmem_limit_bytes=12 * MIB),
        cost_estimate=pl.CostEstimate(
            flops=140_000_000, bytes_accessed=2_000_000, transcendentals=270_000
        ),
    )(*query, *own, *twin)


def spread_kernel(start, att, hid, out_own, out_twin, *rest):
    outs = rest[-NX:]
    size = outs[0].shape[0]
    head = HEAD_DIM
    span = pl.ds(start, NX * size)
    left = jnp.concatenate(
        [att[span, :head], hid[span, : 3 * head], att[span, head:], hid[span, 3 * head :]], axis=1
    )
    right = jnp.concatenate([out_own[...], out_twin[...]], axis=0)
    partial = dot(left, right).astype(BF16)
    for m, out in enumerate(outs):
        out[...] = partial[m * size : (m + 1) * size]


def spread(size, start, att, hid, weights, first):
    depth = weights[0].shape[1]
    return pl.pallas_call(
        functools.partial(spread_kernel, start),
        in_specs=whole(4) + [pl.BlockSpec(memory_space=pl.ANY)] * len(first),
        out_specs=whole(NX),
        out_shape=[jax.ShapeDtypeStruct((size, depth), BF16)] * NX,
        compiler_params=pltpu.CompilerParams(vmem_limit_bytes=16 * MIB),
        cost_estimate=pl.CostEstimate(
            flops=16 * NX * size * depth * HEAD_DIM,
            bytes_accessed=16 * depth * HEAD_DIM + 2 * NX * size * depth,
            transcendentals=0,
        ),
    )(att, hid, *weights, *first)


def added(*parts):
    return sum(p.astype(F32) for p in parts).astype(BF16)


def shards(tokens, ln_gain, w_qkv, q_gain, k_gain, w_up, up_bias, w_out_attn, w_down):
    rows, depth = tokens.shape
    w_qkv = jnp.transpose(w_qkv, (1, 0, 2))
    up_twin, qkv_twin = send(w_up, TWIN), send(w_qkv, TWIN)

    held, left, right, far = {}, {}, {}, {}
    held[0] = norm_rows(tokens, ln_gain)
    next1 = send(held[0], UP)
    left[0] = send(held[0], RIGHT)
    right[0] = send(held[0], LEFT)
    held[1] = gate(gate(next1), left[0], right[0], up_twin, qkv_twin)
    next2 = send(held[1], UP)
    far[0] = send(left[0], RIGHT)
    right[1] = send(held[1], LEFT)
    left[1] = send(held[1], RIGHT)
    far[1] = send(right[1], LEFT)
    held[2] = gate(next2, far[0], right[1])
    next3 = send(held[2], UP)
    left[2] = send(held[2], RIGHT)
    right[2] = send(held[2], LEFT)
    far[2] = send(left[2], RIGHT)
    held[3] = gate(next3, far[1], left[1], left[2], right[2])
    right[3] = send(held[3], LEFT)
    left[3] = send(held[3], RIGHT)
    bias_twin = send(pack(up_bias.shape, (left[1],), up_bias), TWIN)
    out_own = pack(
        (4 * HEAD_DIM, depth), (far[1], left[2], right[2], next3, bias_twin), w_out_attn, w_down
    )
    w_in = (w_qkv, qkv_twin, w_up, up_twin, q_gain, k_gain, up_bias, bias_twin)
    w_out = (out_own, send(out_own, TWIN))

    def rows_of(*blocks):
        return [a[k] for k in blocks for a in (held, left, right, far)]

    *early, kept = project(rows_of(0, 1), w_in, keep=True)
    far[3] = send(gate(right[3], early[0]), LEFT)
    w_in = (w_qkv, kept, *w_in[2:])
    query, own, hidden = zip(early, project(rows_of(2), w_in), project(rows_of(3), w_in))
    twin = [send(part, TWIN) for part in own]
    attended = attend(rows, query, own, twin)

    block_rows = NX * rows
    place = {0: (0, 0), 1: (0, block_rows), 2: (1, 0), 3: (2, 0)}

    def block_sums(k, *first):
        group, start = place[k]
        return spread(rows, start, attended[group], hidden[group], w_out, first)

    mine1, left1, right1, far1 = block_sums(1)
    far1 = send(far1, LEFT)
    from_left1 = send(right1, RIGHT)
    mine2, left2, right2, far2 = block_sums(2, mine1)
    far2 = send(far2, RIGHT)
    from_right1 = send(added(left1, far1), LEFT)
    from_right2 = send(left2, LEFT)
    from_left2 = send(added(right2, far2), RIGHT)
    mine3, left3, right3, far3 = block_sums(3, mine2, far2, far1)
    sum1 = added(mine1, from_left1, from_right1)
    up1 = send(sum1, UP)
    far3 = send(far3, LEFT)
    from_left3 = send(right3, RIGHT)
    mine0, left0, right0, far0 = block_sums(0, mine3)
    far0 = send(gate(far0, sum1), RIGHT)
    from_right3 = send(added(left3, far3), LEFT)
    up2 = send(added(mine2, from_left2, from_right2, up1), UP)
    from_right0 = send(gate(left0, up1), LEFT)
    from_left0 = send(added(right0, far0), RIGHT)
    up3 = send(added(mine3, from_left3, from_right3, up2), UP)
    return added(tokens, mine0, from_left0, from_right0, up3)


def solution(mesh):
    placed = (
        P(("dp", "mp"), None),
        P(),
        P(None, None, "mp"),
        P(),
        P(),
        P(None, "mp"),
        P("mp"),
        P("mp", None),
        P("mp", None),
    )
    return jax.shard_map(
        shards, mesh=mesh, in_specs=placed, out_specs=P(("dp", "mp"), None), check_vma=False
    )
```

```python
import functools
import math

import jax
import jax.numpy as jnp
from jax import lax
from jax.experimental import pallas as pl
from jax.experimental.pallas import tpu as pltpu
from jax.sharding import PartitionSpec as P

HEAD_DIM = 128
NX = 4
NZ = 4
BF16 = jnp.bfloat16
F32 = jnp.float32
MIB = 1 << 20


Z_NEXT = (1, 3, 0, 2)


def moves(dx, up, dc):
    pairs = []
    for x in range(NX):
        for z in range(NZ):
            for c in range(2):
                to = (((x + dx) % NX) * NZ + (Z_NEXT[z] if up else z)) * 2 + (c + dc) % 2
                pairs.append(((x * NZ + z) * 2 + c, to))
    return pairs


RIGHT = moves(1, False, 0)
LEFT = moves(-1, False, 0)
UP = moves(0, True, 0)
TWIN = moves(0, False, 1)


def send(rows, way):
    return lax.ppermute(rows, "mp", way)


def whole(count):
    return [pl.BlockSpec(memory_space=pltpu.VMEM)] * count


def dot(a, b):
    return jnp.dot(a, b, preferred_element_type=F32)


def normalize(rows, gain):
    values = rows.astype(F32)
    mean = jnp.mean(values, axis=-1, keepdims=True)
    centred = values - mean
    spread = jnp.mean(centred * centred, axis=-1, keepdims=True)
    return centred * lax.rsqrt(spread + 1e-06) * gain


def norm_kernel(rows_ref, gain_ref, out_ref):
    out_ref[...] = normalize(rows_ref[...], gain_ref[...].reshape(1, -1)).astype(BF16)


def norm_rows(tokens, gain):
    return pl.pallas_call(
        norm_kernel, out_shape=jax.ShapeDtypeStruct(tokens.shape, BF16)
    )(tokens, gain)


def pack_kernel(skipped, *refs):
    parts, out = refs[skipped:-1], refs[-1]
    at = 0
    for part in parts:
        out[pl.ds(at, part.shape[0])] = part[...]
        at += part.shape[0]


def pack(shape, first, *parts):
    return pl.pallas_call(
        functools.partial(pack_kernel, len(first)),
        in_specs=[pl.BlockSpec(memory_space=pl.ANY)] * len(first) + whole(len(parts)),
        out_specs=pl.BlockSpec(memory_space=pltpu.VMEM),
        out_shape=jax.ShapeDtypeStruct(shape, parts[0].dtype),
        compiler_params=pltpu.CompilerParams(vmem_limit_bytes=11 * MIB),
        cost_estimate=pl.CostEstimate(
            flops=0, bytes_accessed=sum(4 * a.size for a in parts), transcendentals=0
        ),
    )(*first, *parts)


def nothing_kernel(*_):
    pass


def gate(array, *first):
    return pl.pallas_call(
        nothing_kernel,
        in_specs=[pl.BlockSpec(memory_space=pl.ANY)] * (1 + len(first)),
        out_specs=pl.BlockSpec(memory_space=pl.ANY),
        out_shape=jax.ShapeDtypeStruct(array.shape, array.dtype),
        input_output_aliases={0: 0},
        compiler_params=pltpu.CompilerParams(vmem_limit_bytes=MIB),
        cost_estimate=pl.CostEstimate(flops=0, bytes_accessed=0, transcendentals=0),
    )(array, *first)


def project_kernel(count, keep, *refs):
    pieces, rest = refs[:count], refs[count:]
    qkv_own, qkv_twin, up_own, up_twin, q_gain, k_gain, bias_own, bias_twin = rest[:8]
    query, key_value, hidden, *kept, rows = rest[8:]
    if keep:
        kept[0][...] = qkv_twin[...]
    size = pieces[0].shape[0]
    head = HEAD_DIM
    for i, piece in enumerate(pieces):
        rows[pl.ds(i * size, size), :] = piece[...]
    for t, (qkv, up, bias_ref) in enumerate(
        ((qkv_own, up_own, bias_own), (qkv_twin, up_twin, bias_twin))
    ):
        bias = bias_ref[...].reshape(1, -1)
        first = dot(rows[...], jnp.concatenate([qkv[0], qkv[1]], axis=1))
        query[:, t * head : (t + 1) * head] = normalize(
            first[:, :head], q_gain[...].reshape(1, -1)
        ).astype(BF16)
        at = 2 * t * head
        key_value[:, at : at + head] = normalize(
            first[:, head:], k_gain[...].reshape(1, -1)
        ).astype(BF16)
        second = dot(rows[...], jnp.concatenate([qkv[2], up[:, :head]], axis=1))
        key_value[:, at + head : at + 2 * head] = second[:, :head].astype(BF16)
        at = 3 * t * head
        hidden[:, at : at + head] = jax.nn.gelu(second[:, head:] + bias[:, :head]).astype(BF16)
        third = dot(rows[...], up[:, head:])
        hidden[:, at + head : at + 3 * head] = jax.nn.gelu(third + bias[:, head:]).astype(BF16)


def project(pieces, weights, keep=False):
    size, depth = pieces[0].shape
    count = len(pieces) * size
    return pl.pallas_call(
        functools.partial(project_kernel, len(pieces), keep),
        in_specs=whole(len(pieces) + 8),
        out_specs=whole(3 + keep),
        out_shape=[jax.ShapeDtypeStruct((count, n * HEAD_DIM), BF16) for n in (2, 4, 6)]
        + [jax.ShapeDtypeStruct(weights[1].shape, BF16)] * keep,
        scratch_shapes=[pltpu.VMEM((count, depth), BF16)],
        compiler_params=pltpu.CompilerParams(vmem_limit_bytes=24 * MIB),
        cost_estimate=pl.CostEstimate(
            flops=24 * count * depth * HEAD_DIM,
            bytes_accessed=24 * depth * HEAD_DIM + 2 * count * depth,
            transcendentals=6 * count * HEAD_DIM,
        ),
    )(*pieces, *weights)


def stack_rows(pieces, rows):
    size = pieces[0].shape[0]
    for i, piece in enumerate(pieces):
        rows[pl.ds(i * size, size), :] = piece[...]


def heads_kernel(count, *refs):
    qkv_own, qkv_twin, q_gain, k_gain, query, key_value, rows = refs[count:]
    stack_rows(refs[:count], rows)
    head = HEAD_DIM
    value = dot(rows[...], jnp.concatenate([qkv_own[2], qkv_twin[2]], axis=1))
    for t, qkv in enumerate((qkv_own, qkv_twin)):
        both = dot(rows[...], jnp.concatenate([qkv[0], qkv[1]], axis=1))
        query[:, t * head : (t + 1) * head] = normalize(
            both[:, :head], q_gain[...].reshape(1, -1)
        ).astype(BF16)
        at = 2 * t * head
        key_value[:, at : at + head] = normalize(
            both[:, head:], k_gain[...].reshape(1, -1)
        ).astype(BF16)
        key_value[:, at + head : at + 2 * head] = value[:, t * head : (t + 1) * head].astype(BF16)


def hidden_kernel(count, *refs):
    up_own, up_twin, bias_own, bias_twin, hidden, rows = refs[count:]
    stack_rows(refs[:count], rows)
    head = HEAD_DIM
    first = dot(rows[...], jnp.concatenate([up_own[:, :head], up_twin[:, :head]], axis=1))
    for t, (up, bias_ref) in enumerate(((up_own, bias_own), (up_twin, bias_twin))):
        bias = bias_ref[...].reshape(1, -1)
        at = 3 * t * head
        hidden[:, at : at + head] = jax.nn.gelu(
            first[:, t * head : (t + 1) * head] + bias[:, :head]
        ).astype(BF16)
        rest = dot(rows[...], up[:, head:])
        hidden[:, at + head : at + 3 * head] = jax.nn.gelu(rest + bias[:, head:]).astype(BF16)


def project_in_two(pieces, qkv_own, qkv_twin, up_own, up_twin, q_gain, k_gain, bias_own, bias_twin):
    size, depth = pieces[0].shape
    count = len(pieces) * size

    def call(kernel, widths, arrays):
        return pl.pallas_call(
            functools.partial(kernel, len(pieces)),
            in_specs=whole(len(pieces) + len(arrays)),
            out_specs=whole(len(widths)),
            out_shape=[jax.ShapeDtypeStruct((count, n * HEAD_DIM), BF16) for n in widths],
            scratch_shapes=[pltpu.VMEM((count, depth), BF16)],
            compiler_params=pltpu.CompilerParams(vmem_limit_bytes=13 * MIB),
            cost_estimate=pl.CostEstimate(
                flops=12 * count * depth * HEAD_DIM,
                bytes_accessed=12 * depth * HEAD_DIM + 2 * count * depth,
                transcendentals=3 * count * HEAD_DIM,
            ),
        )(*pieces, *arrays)

    query, key_value = call(heads_kernel, (2, 4), (qkv_own, qkv_twin, q_gain, k_gain))
    (hidden,) = call(hidden_kernel, (6,), (up_own, up_twin, bias_own, bias_twin))
    return query, key_value, hidden


def attend_kernel(count, size, *refs):
    query_refs, own_refs, twin_refs = (refs[i * count : (i + 1) * count] for i in range(3))
    out_refs = refs[-count:]

    def image(some, m, at):
        return [
            ref[pl.ds((j * NX + m) * size, size), at : at + HEAD_DIM]
            for ref in some
            for j in range(ref.shape[0] // (NX * size))
        ]

    for m in range(NX):
        for t in range(2):
            own, twin = 2 * t * HEAD_DIM, 2 * (1 - t) * HEAD_DIM
            query = jnp.concatenate(image(query_refs, m, t * HEAD_DIM), axis=0)
            key_rows = jnp.concatenate(image(own_refs, m, own) + image(twin_refs, m, twin), axis=0)
            value = jnp.concatenate(
                image(own_refs, m, own + HEAD_DIM) + image(twin_refs, m, twin + HEAD_DIM), axis=0
            )
            scores = lax.dot_general(
                query, key_rows, (((1,), (1,)), ((), ())), preferred_element_type=F32
            )
            expo = jnp.exp(scores / math.sqrt(HEAD_DIM))
            weights = (expo / jnp.sum(expo, axis=-1, keepdims=True)).astype(BF16)
            mixed = dot(weights, value).astype(BF16)
            at = 0
            for ref in out_refs:
                for j in range(ref.shape[0] // (NX * size)):
                    ref[pl.ds((j * NX + m) * size, size), t * HEAD_DIM : (t + 1) * HEAD_DIM] = mixed[
                        at : at + size
                    ]
                    at += size


def attend(size, query, own, twin, first):
    return pl.pallas_call(
        functools.partial(attend_kernel, len(query), size),
        in_specs=whole(3 * len(query)) + [pl.BlockSpec(memory_space=pl.ANY)],
        out_specs=whole(len(query)),
        out_shape=[jax.ShapeDtypeStruct(a.shape, BF16) for a in query],
        compiler_params=pltpu.CompilerParams(vmem_limit_bytes=12 * MIB),
        cost_estimate=pl.CostEstimate(
            flops=140_000_000, bytes_accessed=2_000_000, transcendentals=270_000
        ),
    )(*query, *own, *twin, first)


def spread_kernel(start, att, hid, out_own, out_twin, *rest):
    outs = rest[-NX:]
    size = outs[0].shape[0]
    head = HEAD_DIM
    span = pl.ds(start, NX * size)
    left = jnp.concatenate(
        [att[span, :head], hid[span, : 3 * head], att[span, head:], hid[span, 3 * head :]], axis=1
    )
    right = jnp.concatenate([out_own[...], out_twin[...]], axis=0)
    partial = dot(left, right).astype(BF16)
    for m, out in enumerate(outs):
        out[...] = partial[m * size : (m + 1) * size]


def spread(size, start, att, hid, weights, first):
    depth = weights[0].shape[1]
    return pl.pallas_call(
        functools.partial(spread_kernel, start),
        in_specs=whole(4) + [pl.BlockSpec(memory_space=pl.ANY)] * len(first),
        out_specs=whole(NX),
        out_shape=[jax.ShapeDtypeStruct((size, depth), BF16)] * NX,
        compiler_params=pltpu.CompilerParams(vmem_limit_bytes=16 * MIB),
        cost_estimate=pl.CostEstimate(
            flops=16 * NX * size * depth * HEAD_DIM,
            bytes_accessed=16 * depth * HEAD_DIM + 2 * NX * size * depth,
            transcendentals=0,
        ),
    )(att, hid, *weights, *first)


def added(*parts):
    return sum(p.astype(F32) for p in parts).astype(BF16)


def shards(tokens, ln_gain, w_qkv, q_gain, k_gain, w_up, up_bias, w_out_attn, w_down):
    rows, depth = tokens.shape
    w_qkv = jnp.transpose(w_qkv, (1, 0, 2))
    up_twin, qkv_twin = send(w_up, TWIN), send(w_qkv, TWIN)

    held, left, right, far = {}, {}, {}, {}
    held[0] = norm_rows(tokens, ln_gain)
    next1 = send(held[0], UP)
    left[0] = send(held[0], RIGHT)
    right[0] = send(held[0], LEFT)
    held[1] = gate(gate(next1), left[0], right[0], up_twin, qkv_twin)
    next2 = send(held[1], UP)
    far[0] = send(left[0], RIGHT)
    right[1] = send(held[1], LEFT)
    left[1] = send(held[1], RIGHT)
    far[1] = send(right[1], LEFT)
    held[2] = gate(next2, far[0], right[1])
    next3 = send(held[2], UP)
    left[2] = send(held[2], RIGHT)
    right[2] = send(held[2], LEFT)
    far[2] = send(left[2], RIGHT)
    held[3] = gate(next3, far[1], left[1], left[2], right[2])
    right[3] = send(held[3], LEFT)
    left[3] = send(held[3], RIGHT)
    bias_twin = send(pack(up_bias.shape, (left[1],), up_bias), TWIN)
    out_own = pack(
        (4 * HEAD_DIM, depth), (far[1], left[2], right[2], next3, bias_twin), w_out_attn, w_down
    )
    w_in = (w_qkv, qkv_twin, w_up, up_twin, q_gain, k_gain, up_bias, bias_twin)
    w_out = (out_own, send(out_own, TWIN))

    def rows_of(*blocks):
        return [a[k] for k in blocks for a in (held, left, right, far)]

    *early, kept = project(rows_of(0, 1), w_in, keep=True)
    far[3] = send(gate(right[3], early[0]), LEFT)
    w_in = (w_qkv, kept, *w_in[2:])
    query, own, hidden = zip(early, project(rows_of(2), w_in), project_in_two(rows_of(3), *w_in))
    twin = [send(part, TWIN) for part in own]
    attended = attend(rows, query, own, twin, hidden[2])

    block_rows = NX * rows
    place = {0: (0, 0), 1: (0, block_rows), 2: (1, 0), 3: (2, 0)}

    def block_sums(k, *first):
        group, start = place[k]
        return spread(rows, start, attended[group], hidden[group], w_out, first)

    mine1, left1, right1, far1 = block_sums(1)
    far1 = send(far1, LEFT)
    from_left1 = send(right1, RIGHT)
    mine2, left2, right2, far2 = block_sums(2, mine1)
    far2 = send(far2, RIGHT)
    from_right1 = send(added(left1, far1), LEFT)
    from_right2 = send(left2, LEFT)
    from_left2 = send(added(right2, far2), RIGHT)
    mine3, left3, right3, far3 = block_sums(3, mine2, far2, far1)
    sum1 = added(mine1, from_left1, from_right1)
    up1 = send(sum1, UP)
    far3 = send(far3, LEFT)
    from_left3 = send(right3, RIGHT)
    mine0, left0, right0, far0 = block_sums(0, mine3)
    far0 = send(gate(far0, sum1), RIGHT)
    from_right3 = send(added(left3, far3), LEFT)
    up2 = send(added(mine2, from_left2, from_right2, up1), UP)
    from_right0 = send(gate(left0, up1), LEFT)
    from_left0 = send(added(right0, far0), RIGHT)
    up3 = send(added(mine3, from_left3, from_right3, up2), UP)
    return added(tokens, mine0, from_left0, from_right0, up3)


def solution(mesh):
    placed = (
        P(("dp", "mp"), None),
        P(),
        P(None, None, "mp"),
        P(),
        P(),
        P(None, "mp"),
        P("mp"),
        P("mp", None),
        P("mp", None),
    )
    return jax.shard_map(
        shards, mesh=mesh, in_specs=placed, out_specs=P(("dp", "mp"), None), check_vma=False
    )
```

```python
import functools
import math

import jax
import jax.numpy as jnp
from jax import lax
from jax.experimental import pallas as pl
from jax.experimental.pallas import tpu as pltpu
from jax.sharding import PartitionSpec as P

HEAD_DIM = 128
NX = 4
NZ = 4
BF16 = jnp.bfloat16
F32 = jnp.float32
MIB = 1 << 20


Z_NEXT = (1, 3, 0, 2)


def moves(dx, up, dc):
    pairs = []
    for x in range(NX):
        for z in range(NZ):
            for c in range(2):
                to = (((x + dx) % NX) * NZ + (Z_NEXT[z] if up else z)) * 2 + (c + dc) % 2
                pairs.append(((x * NZ + z) * 2 + c, to))
    return pairs


RIGHT = moves(1, False, 0)
LEFT = moves(-1, False, 0)
UP = moves(0, True, 0)
TWIN = moves(0, False, 1)


def send(rows, way):
    return lax.ppermute(rows, "mp", way)


def whole(count):
    return [pl.BlockSpec(memory_space=pltpu.VMEM)] * count


def dot(a, b):
    return jnp.dot(a, b, preferred_element_type=F32)


def normalize(rows, gain):
    values = rows.astype(F32)
    mean = jnp.mean(values, axis=-1, keepdims=True)
    centred = values - mean
    spread = jnp.mean(centred * centred, axis=-1, keepdims=True)
    return centred * lax.rsqrt(spread + 1e-06) * gain


def norm_kernel(rows_ref, gain_ref, out_ref):
    out_ref[...] = normalize(rows_ref[...], gain_ref[...].reshape(1, -1)).astype(BF16)


def norm_rows(tokens, gain):
    return pl.pallas_call(
        norm_kernel, out_shape=jax.ShapeDtypeStruct(tokens.shape, BF16)
    )(tokens, gain)


def pack_kernel(skipped, *refs):
    parts, out = refs[skipped:-1], refs[-1]
    at = 0
    for part in parts:
        out[pl.ds(at, part.shape[0])] = part[...]
        at += part.shape[0]


def pack(shape, first, *parts):
    return pl.pallas_call(
        functools.partial(pack_kernel, len(first)),
        in_specs=[pl.BlockSpec(memory_space=pl.ANY)] * len(first) + whole(len(parts)),
        out_specs=pl.BlockSpec(memory_space=pltpu.VMEM),
        out_shape=jax.ShapeDtypeStruct(shape, parts[0].dtype),
        compiler_params=pltpu.CompilerParams(vmem_limit_bytes=11 * MIB),
        cost_estimate=pl.CostEstimate(
            flops=0, bytes_accessed=sum(4 * a.size for a in parts), transcendentals=0
        ),
    )(*first, *parts)


def nothing_kernel(*_):
    pass


def gate(array, *first):
    return pl.pallas_call(
        nothing_kernel,
        in_specs=[pl.BlockSpec(memory_space=pl.ANY)] * (1 + len(first)),
        out_specs=pl.BlockSpec(memory_space=pl.ANY),
        out_shape=jax.ShapeDtypeStruct(array.shape, array.dtype),
        input_output_aliases={0: 0},
        compiler_params=pltpu.CompilerParams(vmem_limit_bytes=MIB),
        cost_estimate=pl.CostEstimate(flops=0, bytes_accessed=0, transcendentals=0),
    )(array, *first)


def part_kernel(start, array_ref, *refs):
    out_ref = refs[-1]
    out_ref[...] = array_ref[pl.ds(start, out_ref.shape[0]), :]


def part(array, start, size, first):
    return pl.pallas_call(
        functools.partial(part_kernel, start),
        in_specs=whole(1) + [pl.BlockSpec(memory_space=pl.ANY)],
        out_specs=pl.BlockSpec(memory_space=pltpu.VMEM),
        out_shape=jax.ShapeDtypeStruct((size, array.shape[1]), array.dtype),
        compiler_params=pltpu.CompilerParams(vmem_limit_bytes=2 * MIB),
        cost_estimate=pl.CostEstimate(flops=0, bytes_accessed=0, transcendentals=0),
    )(array, first)


def project_kernel(count, keep, *refs):
    pieces, rest = refs[:count], refs[count:]
    qkv_own, qkv_twin, up_own, up_twin, q_gain, k_gain, bias_own, bias_twin = rest[:8]
    query, key_value, hidden, *kept, rows = rest[8:]
    if keep:
        kept[0][...] = qkv_twin[...]
    size = pieces[0].shape[0]
    head = HEAD_DIM
    for i, piece in enumerate(pieces):
        rows[pl.ds(i * size, size), :] = piece[...]
    for t, (qkv, up, bias_ref) in enumerate(
        ((qkv_own, up_own, bias_own), (qkv_twin, up_twin, bias_twin))
    ):
        bias = bias_ref[...].reshape(1, -1)
        first = dot(rows[...], jnp.concatenate([qkv[0], qkv[1]], axis=1))
        query[:, t * head : (t + 1) * head] = normalize(
            first[:, :head], q_gain[...].reshape(1, -1)
        ).astype(BF16)
        at = 2 * t * head
        key_value[:, at : at + head] = normalize(
            first[:, head:], k_gain[...].reshape(1, -1)
        ).astype(BF16)
        second = dot(rows[...], jnp.concatenate([qkv[2], up[:, :head]], axis=1))
        key_value[:, at + head : at + 2 * head] = second[:, :head].astype(BF16)
        at = 3 * t * head
        hidden[:, at : at + head] = jax.nn.gelu(second[:, head:] + bias[:, :head]).astype(BF16)
        third = dot(rows[...], up[:, head:])
        hidden[:, at + head : at + 3 * head] = jax.nn.gelu(third + bias[:, head:]).astype(BF16)


def project(pieces, weights, keep=False):
    size, depth = pieces[0].shape
    count = len(pieces) * size
    return pl.pallas_call(
        functools.partial(project_kernel, len(pieces), keep),
        in_specs=whole(len(pieces) + 8),
        out_specs=whole(3 + keep),
        out_shape=[jax.ShapeDtypeStruct((count, n * HEAD_DIM), BF16) for n in (2, 4, 6)]
        + [jax.ShapeDtypeStruct(weights[1].shape, BF16)] * keep,
        scratch_shapes=[pltpu.VMEM((count, depth), BF16)],
        compiler_params=pltpu.CompilerParams(vmem_limit_bytes=24 * MIB),
        cost_estimate=pl.CostEstimate(
            flops=24 * count * depth * HEAD_DIM,
            bytes_accessed=24 * depth * HEAD_DIM + 2 * count * depth,
            transcendentals=6 * count * HEAD_DIM,
        ),
    )(*pieces, *weights)


def stack_rows(pieces, rows):
    at = 0
    for piece in pieces:
        rows[pl.ds(at, piece.shape[0]), :] = piece[...]
        at += piece.shape[0]


def heads_kernel(count, *refs):
    qkv_own, qkv_twin, q_gain, k_gain, query, key_value, rows = refs[count:]
    stack_rows(refs[:count], rows)
    head = HEAD_DIM
    value = dot(rows[...], jnp.concatenate([qkv_own[2], qkv_twin[2]], axis=1))
    for t, qkv in enumerate((qkv_own, qkv_twin)):
        both = dot(rows[...], jnp.concatenate([qkv[0], qkv[1]], axis=1))
        query[:, t * head : (t + 1) * head] = normalize(
            both[:, :head], q_gain[...].reshape(1, -1)
        ).astype(BF16)
        at = 2 * t * head
        key_value[:, at : at + head] = normalize(
            both[:, head:], k_gain[...].reshape(1, -1)
        ).astype(BF16)
        key_value[:, at + head : at + 2 * head] = value[:, t * head : (t + 1) * head].astype(BF16)


def hidden_kernel(count, *refs):
    up_own, up_twin, bias_own, bias_twin, hidden, rows = refs[count:]
    stack_rows(refs[:count], rows)
    head = HEAD_DIM
    first = dot(rows[...], jnp.concatenate([up_own[:, :head], up_twin[:, :head]], axis=1))
    for t, (up, bias_ref) in enumerate(((up_own, bias_own), (up_twin, bias_twin))):
        bias = bias_ref[...].reshape(1, -1)
        at = 3 * t * head
        hidden[:, at : at + head] = jax.nn.gelu(
            first[:, t * head : (t + 1) * head] + bias[:, :head]
        ).astype(BF16)
        rest = dot(rows[...], up[:, head:])
        hidden[:, at + head : at + 3 * head] = jax.nn.gelu(rest + bias[:, head:]).astype(BF16)


def project_in_two(pieces, qkv_own, qkv_twin, up_own, up_twin, q_gain, k_gain, bias_own, bias_twin):
    depth = pieces[0].shape[1]
    count = sum(p.shape[0] for p in pieces)

    def call(kernel, widths, arrays):
        return pl.pallas_call(
            functools.partial(kernel, len(pieces)),
            in_specs=whole(len(pieces) + len(arrays)),
            out_specs=whole(len(widths)),
            out_shape=[jax.ShapeDtypeStruct((count, n * HEAD_DIM), BF16) for n in widths],
            scratch_shapes=[pltpu.VMEM((count, depth), BF16)],
            compiler_params=pltpu.CompilerParams(vmem_limit_bytes=13 * MIB),
            cost_estimate=pl.CostEstimate(
                flops=12 * count * depth * HEAD_DIM,
                bytes_accessed=12 * depth * HEAD_DIM + 2 * count * depth,
                transcendentals=3 * count * HEAD_DIM,
            ),
        )(*pieces, *arrays)

    query, key_value = call(heads_kernel, (2, 4), (qkv_own, qkv_twin, q_gain, k_gain))
    (hidden,) = call(hidden_kernel, (6,), (up_own, up_twin, bias_own, bias_twin))
    return query, key_value, hidden


def attend_kernel(count, size, *refs):
    query_refs, own_refs, twin_refs = (refs[i * count : (i + 1) * count] for i in range(3))
    out_refs = refs[-count:]

    def image(some, m, at):
        return [
            ref[pl.ds((j * NX + m) * size, size), at : at + HEAD_DIM]
            for ref in some
            for j in range(ref.shape[0] // (NX * size))
        ]

    for m in range(NX):
        for t in range(2):
            own, twin = 2 * t * HEAD_DIM, 2 * (1 - t) * HEAD_DIM
            query = jnp.concatenate(image(query_refs, m, t * HEAD_DIM), axis=0)
            key_rows = jnp.concatenate(image(own_refs, m, own) + image(twin_refs, m, twin), axis=0)
            value = jnp.concatenate(
                image(own_refs, m, own + HEAD_DIM) + image(twin_refs, m, twin + HEAD_DIM), axis=0
            )
            scores = lax.dot_general(
                query, key_rows, (((1,), (1,)), ((), ())), preferred_element_type=F32
            )
            expo = jnp.exp(scores / math.sqrt(HEAD_DIM))
            weights = (expo / jnp.sum(expo, axis=-1, keepdims=True)).astype(BF16)
            mixed = dot(weights, value).astype(BF16)
            at = 0
            for ref in out_refs:
                for j in range(ref.shape[0] // (NX * size)):
                    ref[pl.ds((j * NX + m) * size, size), t * HEAD_DIM : (t + 1) * HEAD_DIM] = mixed[
                        at : at + size
                    ]
                    at += size


def attend(size, query, own, twin, first):
    return pl.pallas_call(
        functools.partial(attend_kernel, len(query), size),
        in_specs=whole(3 * len(query)) + [pl.BlockSpec(memory_space=pl.ANY)],
        out_specs=whole(len(query)),
        out_shape=[jax.ShapeDtypeStruct(a.shape, BF16) for a in query],
        compiler_params=pltpu.CompilerParams(vmem_limit_bytes=12 * MIB),
        cost_estimate=pl.CostEstimate(
            flops=140_000_000, bytes_accessed=2_000_000, transcendentals=270_000
        ),
    )(*query, *own, *twin, first)


def spread_kernel(start, att, hid, out_own, out_twin, *rest):
    outs = rest[-NX:]
    size = outs[0].shape[0]
    head = HEAD_DIM
    span = pl.ds(start, NX * size)
    left = jnp.concatenate(
        [att[span, :head], hid[span, : 3 * head], att[span, head:], hid[span, 3 * head :]], axis=1
    )
    right = jnp.concatenate([out_own[...], out_twin[...]], axis=0)
    partial = dot(left, right).astype(BF16)
    for m, out in enumerate(outs):
        out[...] = partial[m * size : (m + 1) * size]


def spread(size, start, att, hid, weights, first):
    depth = weights[0].shape[1]
    return pl.pallas_call(
        functools.partial(spread_kernel, start),
        in_specs=whole(4) + [pl.BlockSpec(memory_space=pl.ANY)] * len(first),
        out_specs=whole(NX),
        out_shape=[jax.ShapeDtypeStruct((size, depth), BF16)] * NX,
        compiler_params=pltpu.CompilerParams(vmem_limit_bytes=16 * MIB),
        cost_estimate=pl.CostEstimate(
            flops=16 * NX * size * depth * HEAD_DIM,
            bytes_accessed=16 * depth * HEAD_DIM + 2 * NX * size * depth,
            transcendentals=0,
        ),
    )(att, hid, *weights, *first)


def added(*parts):
    return sum(p.astype(F32) for p in parts).astype(BF16)


def shards(tokens, ln_gain, w_qkv, q_gain, k_gain, w_up, up_bias, w_out_attn, w_down):
    rows, depth = tokens.shape
    w_qkv = jnp.transpose(w_qkv, (1, 0, 2))
    up_twin, qkv_twin = send(w_up, TWIN), send(w_qkv, TWIN)

    held, left, right, far = {}, {}, {}, {}
    held[0] = norm_rows(tokens, ln_gain)
    next1 = send(held[0], UP)
    left[0] = send(held[0], RIGHT)
    right[0] = send(held[0], LEFT)
    held[1] = gate(gate(next1), left[0], right[0], up_twin, qkv_twin)
    next2 = send(held[1], UP)
    far[0] = send(left[0], RIGHT)
    right[1] = send(held[1], LEFT)
    left[1] = send(held[1], RIGHT)
    far[1] = send(right[1], LEFT)
    held[2] = gate(next2, far[0], right[1])
    next3 = send(held[2], UP)
    left[2] = send(held[2], RIGHT)
    right[2] = send(held[2], LEFT)
    far[2] = send(left[2], RIGHT)
    held[3] = gate(next3, far[1], left[1], left[2], right[2])
    right[3] = send(held[3], LEFT)
    left[3] = send(held[3], RIGHT)
    bias_twin = send(pack(up_bias.shape, (left[1],), up_bias), TWIN)
    out_own = pack(
        (4 * HEAD_DIM, depth), (far[1], left[2], right[2], next3, bias_twin), w_out_attn, w_down
    )
    w_in = (w_qkv, qkv_twin, w_up, up_twin, q_gain, k_gain, up_bias, bias_twin)
    w_out = (out_own, send(out_own, TWIN))

    def rows_of(*blocks):
        return [a[k] for k in blocks for a in (held, left, right, far)]

    *early, kept = project(rows_of(0, 1), w_in, keep=True)
    half = rows // 2
    far_top = send(part(left[3], 0, half, early[0]), RIGHT)
    far_bottom = send(part(right[3], half, half, early[0]), LEFT)
    w_in = (w_qkv, kept, *w_in[2:])
    last = [held[3], left[3], right[3], far_top, far_bottom]
    query, own, hidden = zip(early, project(rows_of(2), w_in), project_in_two(last, *w_in))
    twin = [send(part, TWIN) for part in own]
    attended = attend(rows, query, own, twin, hidden[2])

    block_rows = NX * rows
    place = {0: (0, 0), 1: (0, block_rows), 2: (1, 0), 3: (2, 0)}

    def block_sums(k, *first):
        group, start = place[k]
        return spread(rows, start, attended[group], hidden[group], w_out, first)

    mine1, left1, right1, far1 = block_sums(1)
    far1 = send(far1, LEFT)
    from_left1 = send(right1, RIGHT)
    mine2, left2, right2, far2 = block_sums(2, mine1)
    far2 = send(far2, RIGHT)
    from_right1 = send(added(left1, far1), LEFT)
    from_right2 = send(left2, LEFT)
    from_left2 = send(added(right2, far2), RIGHT)
    mine3, left3, right3, far3 = block_sums(3, mine2, far2, far1)
    sum1 = added(mine1, from_left1, from_right1)
    up1 = send(sum1, UP)
    far3 = send(far3, LEFT)
    from_left3 = send(right3, RIGHT)
    mine0, left0, right0, far0 = block_sums(0, mine3)
    far0 = send(gate(far0, sum1), RIGHT)
    from_right3 = send(added(left3, far3), LEFT)
    up2 = send(added(mine2, from_left2, from_right2, up1), UP)
    from_right0 = send(gate(left0, up1), LEFT)
    from_left0 = send(added(right0, far0), RIGHT)
    up3 = send(added(mine3, from_left3, from_right3, up2), UP)
    return added(tokens, mine0, from_left0, from_right0, up3)


def solution(mesh):
    placed = (
        P(("dp", "mp"), None),
        P(),
        P(None, None, "mp"),
        P(),
        P(),
        P(None, "mp"),
        P("mp"),
        P("mp", None),
        P("mp", None),
    )
    return jax.shard_map(
        shards, mesh=mesh, in_specs=placed, out_specs=P(("dp", "mp"), None), check_vma=False
    )
```

```python
import functools
import math

import jax
import jax.numpy as jnp
from jax import lax
from jax.experimental import pallas as pl
from jax.experimental.pallas import tpu as pltpu
from jax.sharding import PartitionSpec as P

HEAD_DIM = 128
NX = 4
NZ = 4
BF16 = jnp.bfloat16
F32 = jnp.float32
MIB = 1 << 20


Z_NEXT = (1, 3, 0, 2)


def moves(dx, up, dc):
    pairs = []
    for x in range(NX):
        for z in range(NZ):
            for c in range(2):
                to = (((x + dx) % NX) * NZ + (Z_NEXT[z] if up else z)) * 2 + (c + dc) % 2
                pairs.append(((x * NZ + z) * 2 + c, to))
    return pairs


RIGHT = moves(1, False, 0)
LEFT = moves(-1, False, 0)
UP = moves(0, True, 0)
TWIN = moves(0, False, 1)


def send(rows, way):
    return lax.ppermute(rows, "mp", way)


def whole(count):
    return [pl.BlockSpec(memory_space=pltpu.VMEM)] * count


def dot(a, b):
    return jnp.dot(a, b, preferred_element_type=F32)


def normalize(rows, gain):
    values = rows.astype(F32)
    mean = jnp.mean(values, axis=-1, keepdims=True)
    centred = values - mean
    spread = jnp.mean(centred * centred, axis=-1, keepdims=True)
    return centred * lax.rsqrt(spread + 1e-06) * gain


def norm_kernel(rows_ref, gain_ref, out_ref):
    out_ref[...] = normalize(rows_ref[...], gain_ref[...].reshape(1, -1)).astype(BF16)


def norm_rows(tokens, gain):
    return pl.pallas_call(
        norm_kernel,
        out_shape=jax.ShapeDtypeStruct(tokens.shape, BF16),
        compiler_params=pltpu.CompilerParams(vmem_limit_bytes=4 * MIB),
    )(tokens, gain)


def pack_kernel(skipped, *refs):
    parts, out = refs[skipped:-1], refs[-1]
    at = 0
    for part in parts:
        out[pl.ds(at, part.shape[0])] = part[...]
        at += part.shape[0]


def pack(shape, first, *parts):
    return pl.pallas_call(
        functools.partial(pack_kernel, len(first)),
        in_specs=[pl.BlockSpec(memory_space=pl.ANY)] * len(first) + whole(len(parts)),
        out_specs=pl.BlockSpec(memory_space=pltpu.VMEM),
        out_shape=jax.ShapeDtypeStruct(shape, parts[0].dtype),
        compiler_params=pltpu.CompilerParams(vmem_limit_bytes=11 * MIB),
        cost_estimate=pl.CostEstimate(
            flops=0, bytes_accessed=sum(4 * a.size for a in parts), transcendentals=0
        ),
    )(*first, *parts)


def nothing_kernel(*_):
    pass


def gate(array, *first):
    return pl.pallas_call(
        nothing_kernel,
        in_specs=[pl.BlockSpec(memory_space=pl.ANY)] * (1 + len(first)),
        out_specs=pl.BlockSpec(memory_space=pl.ANY),
        out_shape=jax.ShapeDtypeStruct(array.shape, array.dtype),
        input_output_aliases={0: 0},
        compiler_params=pltpu.CompilerParams(vmem_limit_bytes=MIB),
        cost_estimate=pl.CostEstimate(flops=0, bytes_accessed=0, transcendentals=0),
    )(array, *first)


def part_kernel(start, array_ref, *refs):
    out_ref = refs[-1]
    out_ref[...] = array_ref[pl.ds(start, out_ref.shape[0]), :]


def part(array, start, size, first):
    return pl.pallas_call(
        functools.partial(part_kernel, start),
        in_specs=whole(1) + [pl.BlockSpec(memory_space=pl.ANY)],
        out_specs=pl.BlockSpec(memory_space=pltpu.VMEM),
        out_shape=jax.ShapeDtypeStruct((size, array.shape[1]), array.dtype),
        compiler_params=pltpu.CompilerParams(vmem_limit_bytes=2 * MIB),
        cost_estimate=pl.CostEstimate(flops=0, bytes_accessed=0, transcendentals=0),
    )(array, first)


def project_kernel(count, keep, *refs):
    pieces, rest = refs[:count], refs[count:]
    qkv_own, qkv_twin, up_own, up_twin, q_gain, k_gain, bias_own, bias_twin = rest[:8]
    query, key_value, hidden, *kept, rows = rest[8:]
    if keep:
        kept[0][...] = qkv_twin[...]
    size = pieces[0].shape[0]
    head = HEAD_DIM
    for i, piece in enumerate(pieces):
        rows[pl.ds(i * size, size), :] = piece[...]
    for t, (qkv, up, bias_ref) in enumerate(
        ((qkv_own, up_own, bias_own), (qkv_twin, up_twin, bias_twin))
    ):
        bias = bias_ref[...].reshape(1, -1)
        first = dot(rows[...], jnp.concatenate([qkv[0], qkv[1]], axis=1))
        query[:, t * head : (t + 1) * head] = normalize(
            first[:, :head], q_gain[...].reshape(1, -1)
        ).astype(BF16)
        at = 2 * t * head
        key_value[:, at : at + head] = normalize(
            first[:, head:], k_gain[...].reshape(1, -1)
        ).astype(BF16)
        second = dot(rows[...], jnp.concatenate([qkv[2], up[:, :head]], axis=1))
        key_value[:, at + head : at + 2 * head] = second[:, :head].astype(BF16)
        at = 3 * t * head
        hidden[:, at : at + head] = jax.nn.gelu(second[:, head:] + bias[:, :head]).astype(BF16)
        third = dot(rows[...], up[:, head:])
        hidden[:, at + head : at + 3 * head] = jax.nn.gelu(third + bias[:, head:]).astype(BF16)


def project(pieces, weights, keep=False):
    size, depth = pieces[0].shape
    count = len(pieces) * size
    return pl.pallas_call(
        functools.partial(project_kernel, len(pieces), keep),
        in_specs=whole(len(pieces) + 8),
        out_specs=whole(3 + keep),
        out_shape=[jax.ShapeDtypeStruct((count, n * HEAD_DIM), BF16) for n in (2, 4, 6)]
        + [jax.ShapeDtypeStruct(weights[1].shape, BF16)] * keep,
        scratch_shapes=[pltpu.VMEM((count, depth), BF16)],
        compiler_params=pltpu.CompilerParams(vmem_limit_bytes=24 * MIB),
        cost_estimate=pl.CostEstimate(
            flops=24 * count * depth * HEAD_DIM,
            bytes_accessed=24 * depth * HEAD_DIM + 2 * count * depth,
            transcendentals=6 * count * HEAD_DIM,
        ),
    )(*pieces, *weights)


def stack_rows(pieces, rows):
    at = 0
    for piece in pieces:
        rows[pl.ds(at, piece.shape[0]), :] = piece[...]
        at += piece.shape[0]


def heads_kernel(count, *refs):
    qkv_own, qkv_twin, q_gain, k_gain, query, key_value, rows = refs[count:]
    stack_rows(refs[:count], rows)
    head = HEAD_DIM
    value = dot(rows[...], jnp.concatenate([qkv_own[2], qkv_twin[2]], axis=1))
    for t, qkv in enumerate((qkv_own, qkv_twin)):
        both = dot(rows[...], jnp.concatenate([qkv[0], qkv[1]], axis=1))
        query[:, t * head : (t + 1) * head] = normalize(
            both[:, :head], q_gain[...].reshape(1, -1)
        ).astype(BF16)
        at = 2 * t * head
        key_value[:, at : at + head] = normalize(
            both[:, head:], k_gain[...].reshape(1, -1)
        ).astype(BF16)
        key_value[:, at + head : at + 2 * head] = value[:, t * head : (t + 1) * head].astype(BF16)


def hidden_kernel(count, *refs):
    up_own, up_twin, bias_own, bias_twin, hidden, rows = refs[count:]
    stack_rows(refs[:count], rows)
    head = HEAD_DIM
    first = dot(rows[...], jnp.concatenate([up_own[:, :head], up_twin[:, :head]], axis=1))
    for t, (up, bias_ref) in enumerate(((up_own, bias_own), (up_twin, bias_twin))):
        bias = bias_ref[...].reshape(1, -1)
        at = 3 * t * head
        hidden[:, at : at + head] = jax.nn.gelu(
            first[:, t * head : (t + 1) * head] + bias[:, :head]
        ).astype(BF16)
        rest = dot(rows[...], up[:, head:])
        hidden[:, at + head : at + 3 * head] = jax.nn.gelu(rest + bias[:, head:]).astype(BF16)


def project_in_two(pieces, qkv_own, qkv_twin, up_own, up_twin, q_gain, k_gain, bias_own, bias_twin):
    depth = pieces[0].shape[1]
    count = sum(p.shape[0] for p in pieces)

    def call(kernel, widths, arrays):
        return pl.pallas_call(
            functools.partial(kernel, len(pieces)),
            in_specs=whole(len(pieces) + len(arrays)),
            out_specs=whole(len(widths)),
            out_shape=[jax.ShapeDtypeStruct((count, n * HEAD_DIM), BF16) for n in widths],
            scratch_shapes=[pltpu.VMEM((count, depth), BF16)],
            compiler_params=pltpu.CompilerParams(vmem_limit_bytes=13 * MIB),
            cost_estimate=pl.CostEstimate(
                flops=12 * count * depth * HEAD_DIM,
                bytes_accessed=12 * depth * HEAD_DIM + 2 * count * depth,
                transcendentals=3 * count * HEAD_DIM,
            ),
        )(*pieces, *arrays)

    query, key_value = call(heads_kernel, (2, 4), (qkv_own, qkv_twin, q_gain, k_gain))
    (hidden,) = call(hidden_kernel, (6,), (up_own, up_twin, bias_own, bias_twin))
    return query, key_value, hidden


def attend_kernel(count, size, *refs):
    query_refs, own_refs, twin_refs = (refs[i * count : (i + 1) * count] for i in range(3))
    out_refs = refs[-count:]

    def image(some, m, at):
        return [
            ref[pl.ds((j * NX + m) * size, size), at : at + HEAD_DIM]
            for ref in some
            for j in range(ref.shape[0] // (NX * size))
        ]

    for m in range(NX):
        for t in range(2):
            own, twin = 2 * t * HEAD_DIM, 2 * (1 - t) * HEAD_DIM
            query = jnp.concatenate(image(query_refs, m, t * HEAD_DIM), axis=0)
            key_rows = jnp.concatenate(image(own_refs, m, own) + image(twin_refs, m, twin), axis=0)
            value = jnp.concatenate(
                image(own_refs, m, own + HEAD_DIM) + image(twin_refs, m, twin + HEAD_DIM), axis=0
            )
            scores = lax.dot_general(
                query, key_rows, (((1,), (1,)), ((), ())), preferred_element_type=F32
            )
            expo = jnp.exp(scores / math.sqrt(HEAD_DIM))
            weights = (expo / jnp.sum(expo, axis=-1, keepdims=True)).astype(BF16)
            mixed = dot(weights, value).astype(BF16)
            at = 0
            for ref in out_refs:
                for j in range(ref.shape[0] // (NX * size)):
                    ref[pl.ds((j * NX + m) * size, size), t * HEAD_DIM : (t + 1) * HEAD_DIM] = mixed[
                        at : at + size
                    ]
                    at += size


def attend(size, query, own, twin, first):
    return pl.pallas_call(
        functools.partial(attend_kernel, len(query), size),
        in_specs=whole(3 * len(query)) + [pl.BlockSpec(memory_space=pl.ANY)],
        out_specs=whole(len(query)),
        out_shape=[jax.ShapeDtypeStruct(a.shape, BF16) for a in query],
        compiler_params=pltpu.CompilerParams(vmem_limit_bytes=12 * MIB),
        cost_estimate=pl.CostEstimate(
            flops=140_000_000, bytes_accessed=2_000_000, transcendentals=270_000
        ),
    )(*query, *own, *twin, first)


def spread_kernel(start, att, hid, out_own, out_twin, *rest):
    outs = rest[-NX:]
    size = outs[0].shape[0]
    head = HEAD_DIM
    span = pl.ds(start, NX * size)
    left = jnp.concatenate(
        [att[span, :head], hid[span, : 3 * head], att[span, head:], hid[span, 3 * head :]], axis=1
    )
    right = jnp.concatenate([out_own[...], out_twin[...]], axis=0)
    partial = dot(left, right).astype(BF16)
    for m, out in enumerate(outs):
        out[...] = partial[m * size : (m + 1) * size]


def spread(size, start, att, hid, weights, first):
    depth = weights[0].shape[1]
    return pl.pallas_call(
        functools.partial(spread_kernel, start),
        in_specs=whole(4) + [pl.BlockSpec(memory_space=pl.ANY)] * len(first),
        out_specs=whole(NX),
        out_shape=[jax.ShapeDtypeStruct((size, depth), BF16)] * NX,
        compiler_params=pltpu.CompilerParams(vmem_limit_bytes=16 * MIB),
        cost_estimate=pl.CostEstimate(
            flops=16 * NX * size * depth * HEAD_DIM,
            bytes_accessed=16 * depth * HEAD_DIM + 2 * NX * size * depth,
            transcendentals=0,
        ),
    )(att, hid, *weights, *first)


def added(*parts):
    return sum(p.astype(F32) for p in parts).astype(BF16)


def shards(tokens, ln_gain, w_qkv, q_gain, k_gain, w_up, up_bias, w_out_attn, w_down):
    rows, depth = tokens.shape
    w_qkv = jnp.transpose(w_qkv, (1, 0, 2))
    up_twin, qkv_twin = send(w_up, TWIN), send(w_qkv, TWIN)

    held, left, right, far = {}, {}, {}, {}
    held[0] = norm_rows(tokens, ln_gain)
    next1 = send(held[0], UP)
    left[0] = send(held[0], RIGHT)
    right[0] = send(held[0], LEFT)
    held[1] = gate(gate(next1), left[0], right[0], up_twin, qkv_twin)
    next2 = send(held[1], UP)
    far[0] = send(left[0], RIGHT)
    right[1] = send(held[1], LEFT)
    left[1] = send(held[1], RIGHT)
    far[1] = send(right[1], LEFT)
    held[2] = gate(next2, far[0], right[1])
    next3 = send(held[2], UP)
    left[2] = send(held[2], RIGHT)
    right[2] = send(held[2], LEFT)
    far[2] = send(left[2], RIGHT)
    held[3] = gate(next3, far[1], left[1], left[2], right[2])
    right[3] = send(held[3], LEFT)
    left[3] = send(held[3], RIGHT)
    bias_twin = send(pack(up_bias.shape, (left[1],), up_bias), TWIN)
    out_own = pack(
        (4 * HEAD_DIM, depth), (far[1], left[2], right[2], next3, bias_twin), w_out_attn, w_down
    )
    w_in = (w_qkv, qkv_twin, w_up, up_twin, q_gain, k_gain, up_bias, bias_twin)
    w_out = (out_own, send(out_own, TWIN))

    def rows_of(*blocks):
        return [a[k] for k in blocks for a in (held, left, right, far)]

    *early, kept = project(rows_of(0, 1), w_in, keep=True)
    half = rows // 2
    far_top = send(part(left[3], 0, half, early[0]), RIGHT)
    far_bottom = send(part(right[3], half, half, early[0]), LEFT)
    w_in = (w_qkv, kept, *w_in[2:])
    last = [held[3], left[3], right[3], far_top, far_bottom]
    query, own, hidden = zip(early, project(rows_of(2), w_in), project_in_two(last, *w_in))
    twin = [send(part, TWIN) for part in own]
    attended = attend(rows, query, own, twin, hidden[2])

    block_rows = NX * rows
    place = {0: (0, 0), 1: (0, block_rows), 2: (1, 0), 3: (2, 0)}

    def block_sums(k, *first):
        group, start = place[k]
        return spread(rows, start, attended[group], hidden[group], w_out, first)

    mine1, left1, right1, far1 = block_sums(1)
    far1 = send(far1, LEFT)
    from_left1 = send(right1, RIGHT)
    mine2, left2, right2, far2 = block_sums(2, mine1)
    far2 = send(far2, RIGHT)
    from_right1 = send(added(left1, far1), LEFT)
    from_right2 = send(left2, LEFT)
    from_left2 = send(added(right2, far2), RIGHT)
    mine3, left3, right3, far3 = block_sums(3, mine2, far2, far1)
    sum1 = added(mine1, from_left1, from_right1)
    up1 = send(sum1, UP)
    far3 = send(far3, LEFT)
    from_left3 = send(right3, RIGHT)
    mine0, left0, right0, far0 = block_sums(0, mine3)
    far0 = send(gate(far0, sum1), RIGHT)
    from_right3 = send(added(left3, far3), LEFT)
    up2 = send(added(mine2, from_left2, from_right2, up1), UP)
    from_right0 = send(gate(left0, up1), LEFT)
    from_left0 = send(added(right0, far0), RIGHT)
    up3 = send(added(mine3, from_left3, from_right3, up2), UP)
    return added(tokens, mine0, from_left0, from_right0, up3)


def solution(mesh):
    placed = (
        P(("dp", "mp"), None),
        P(),
        P(None, None, "mp"),
        P(),
        P(),
        P(None, "mp"),
        P("mp"),
        P("mp", None),
        P("mp", None),
    )
    return jax.shard_map(
        shards, mesh=mesh, in_specs=placed, out_specs=P(("dp", "mp"), None), check_vma=False
    )
```

```python
import functools
import math

import jax
import jax.numpy as jnp
from jax import lax
from jax.experimental import pallas as pl
from jax.experimental.pallas import tpu as pltpu
from jax.sharding import PartitionSpec as P

HEAD_DIM = 128
NX = 4
NZ = 4
BF16 = jnp.bfloat16
F32 = jnp.float32
MIB = 1 << 20


Z_NEXT = (1, 3, 0, 2)


def moves(dx, up, dc):
    pairs = []
    for x in range(NX):
        for z in range(NZ):
            for c in range(2):
                to = (((x + dx) % NX) * NZ + (Z_NEXT[z] if up else z)) * 2 + (c + dc) % 2
                pairs.append(((x * NZ + z) * 2 + c, to))
    return pairs


RIGHT = moves(1, False, 0)
LEFT = moves(-1, False, 0)
UP = moves(0, True, 0)
TWIN = moves(0, False, 1)


def send(rows, way):
    return lax.ppermute(rows, "mp", way)


def whole(count):
    return [pl.BlockSpec(memory_space=pltpu.VMEM)] * count


def dot(a, b):
    return jnp.dot(a, b, preferred_element_type=F32)


def normalize(rows, gain):
    values = rows.astype(F32)
    mean = jnp.mean(values, axis=-1, keepdims=True)
    centred = values - mean
    spread = jnp.mean(centred * centred, axis=-1, keepdims=True)
    return centred * lax.rsqrt(spread + 1e-06) * gain


def norm_kernel(rows_ref, gain_ref, out_ref):
    out_ref[...] = normalize(rows_ref[...], gain_ref[...].reshape(1, -1)).astype(BF16)


def norm_rows(tokens, gain):
    return pl.pallas_call(
        norm_kernel, out_shape=jax.ShapeDtypeStruct(tokens.shape, BF16)
    )(tokens, gain)


def pack_kernel(skipped, *refs):
    parts, out = refs[skipped:-1], refs[-1]
    at = 0
    for part in parts:
        out[pl.ds(at, part.shape[0])] = part[...]
        at += part.shape[0]


def pack(shape, first, *parts):
    return pl.pallas_call(
        functools.partial(pack_kernel, len(first)),
        in_specs=[pl.BlockSpec(memory_space=pl.ANY)] * len(first) + whole(len(parts)),
        out_specs=pl.BlockSpec(memory_space=pltpu.VMEM),
        out_shape=jax.ShapeDtypeStruct(shape, parts[0].dtype),
        compiler_params=pltpu.CompilerParams(vmem_limit_bytes=11 * MIB),
        cost_estimate=pl.CostEstimate(
            flops=0, bytes_accessed=sum(4 * a.size for a in parts), transcendentals=0
        ),
    )(*first, *parts)


def nothing_kernel(*_):
    pass


def gate(array, *first):
    return pl.pallas_call(
        nothing_kernel,
        in_specs=[pl.BlockSpec(memory_space=pl.ANY)] * (1 + len(first)),
        out_specs=pl.BlockSpec(memory_space=pl.ANY),
        out_shape=jax.ShapeDtypeStruct(array.shape, array.dtype),
        input_output_aliases={0: 0},
        compiler_params=pltpu.CompilerParams(vmem_limit_bytes=MIB),
        cost_estimate=pl.CostEstimate(flops=0, bytes_accessed=0, transcendentals=0),
    )(array, *first)


def part_kernel(start, array_ref, *refs):
    out_ref = refs[-1]
    out_ref[...] = array_ref[pl.ds(start, out_ref.shape[0]), :]


def part(array, start, size, first):
    return pl.pallas_call(
        functools.partial(part_kernel, start),
        in_specs=whole(1) + [pl.BlockSpec(memory_space=pl.ANY)],
        out_specs=pl.BlockSpec(memory_space=pltpu.VMEM),
        out_shape=jax.ShapeDtypeStruct((size, array.shape[1]), array.dtype),
        compiler_params=pltpu.CompilerParams(vmem_limit_bytes=2 * MIB),
        cost_estimate=pl.CostEstimate(flops=0, bytes_accessed=0, transcendentals=0),
    )(array, first)


def project_kernel(count, keep, *refs):
    pieces, rest = refs[:count], refs[count:]
    qkv_own, qkv_twin, up_own, up_twin, q_gain, k_gain, bias_own, bias_twin = rest[:8]
    query, key_value, hidden, *kept, rows = rest[8:]
    if keep:
        kept[0][...] = qkv_twin[...]
    size = pieces[0].shape[0]
    head = HEAD_DIM
    for i, piece in enumerate(pieces):
        rows[pl.ds(i * size, size), :] = piece[...]
    for t, (qkv, up, bias_ref) in enumerate(
        ((qkv_own, up_own, bias_own), (qkv_twin, up_twin, bias_twin))
    ):
        bias = bias_ref[...].reshape(1, -1)
        first = dot(rows[...], jnp.concatenate([qkv[0], qkv[1]], axis=1))
        query[:, t * head : (t + 1) * head] = normalize(
            first[:, :head], q_gain[...].reshape(1, -1)
        ).astype(BF16)
        at = 2 * t * head
        key_value[:, at : at + head] = normalize(
            first[:, head:], k_gain[...].reshape(1, -1)
        ).astype(BF16)
        second = dot(rows[...], jnp.concatenate([qkv[2], up[:, :head]], axis=1))
        key_value[:, at + head : at + 2 * head] = second[:, :head].astype(BF16)
        at = 3 * t * head
        hidden[:, at : at + head] = jax.nn.gelu(second[:, head:] + bias[:, :head]).astype(BF16)
        third = dot(rows[...], up[:, head:])
        hidden[:, at + head : at + 3 * head] = jax.nn.gelu(third + bias[:, head:]).astype(BF16)


def project(pieces, weights, keep=False):
    size, depth = pieces[0].shape
    count = len(pieces) * size
    return pl.pallas_call(
        functools.partial(project_kernel, len(pieces), keep),
        in_specs=whole(len(pieces) + 8),
        out_specs=whole(3 + keep),
        out_shape=[jax.ShapeDtypeStruct((count, n * HEAD_DIM), BF16) for n in (2, 4, 6)]
        + [jax.ShapeDtypeStruct(weights[1].shape, BF16)] * keep,
        scratch_shapes=[pltpu.VMEM((count, depth), BF16)],
        compiler_params=pltpu.CompilerParams(vmem_limit_bytes=24 * MIB),
        cost_estimate=pl.CostEstimate(
            flops=24 * count * depth * HEAD_DIM,
            bytes_accessed=24 * depth * HEAD_DIM + 2 * count * depth,
            transcendentals=6 * count * HEAD_DIM,
        ),
    )(*pieces, *weights)


def stack_rows(pieces, rows):
    at = 0
    for piece in pieces:
        rows[pl.ds(at, piece.shape[0]), :] = piece[...]
        at += piece.shape[0]


def heads_kernel(count, *refs):
    qkv_own, qkv_twin, q_gain, k_gain, query, key_value, rows = refs[count:]
    stack_rows(refs[:count], rows)
    head = HEAD_DIM
    value = dot(rows[...], jnp.concatenate([qkv_own[2], qkv_twin[2]], axis=1))
    for t, qkv in enumerate((qkv_own, qkv_twin)):
        both = dot(rows[...], jnp.concatenate([qkv[0], qkv[1]], axis=1))
        query[:, t * head : (t + 1) * head] = normalize(
            both[:, :head], q_gain[...].reshape(1, -1)
        ).astype(BF16)
        at = 2 * t * head
        key_value[:, at : at + head] = normalize(
            both[:, head:], k_gain[...].reshape(1, -1)
        ).astype(BF16)
        key_value[:, at + head : at + 2 * head] = value[:, t * head : (t + 1) * head].astype(BF16)


def hidden_kernel(count, *refs):
    up_own, up_twin, bias_own, bias_twin, hidden, rows = refs[count:]
    stack_rows(refs[:count], rows)
    head = HEAD_DIM
    first = dot(rows[...], jnp.concatenate([up_own[:, :head], up_twin[:, :head]], axis=1))
    for t, (up, bias_ref) in enumerate(((up_own, bias_own), (up_twin, bias_twin))):
        bias = bias_ref[...].reshape(1, -1)
        at = 3 * t * head
        hidden[:, at : at + head] = jax.nn.gelu(
            first[:, t * head : (t + 1) * head] + bias[:, :head]
        ).astype(BF16)
        rest = dot(rows[...], up[:, head:])
        hidden[:, at + head : at + 3 * head] = jax.nn.gelu(rest + bias[:, head:]).astype(BF16)


def project_in_two(pieces, qkv_own, qkv_twin, up_own, up_twin, q_gain, k_gain, bias_own, bias_twin):
    depth = pieces[0].shape[1]
    count = sum(p.shape[0] for p in pieces)

    def call(kernel, widths, arrays):
        return pl.pallas_call(
            functools.partial(kernel, len(pieces)),
            in_specs=whole(len(pieces) + len(arrays)),
            out_specs=whole(len(widths)),
            out_shape=[jax.ShapeDtypeStruct((count, n * HEAD_DIM), BF16) for n in widths],
            scratch_shapes=[pltpu.VMEM((count, depth), BF16)],
            compiler_params=pltpu.CompilerParams(vmem_limit_bytes=13 * MIB),
            cost_estimate=pl.CostEstimate(
                flops=12 * count * depth * HEAD_DIM,
                bytes_accessed=12 * depth * HEAD_DIM + 2 * count * depth,
                transcendentals=3 * count * HEAD_DIM,
            ),
        )(*pieces, *arrays)

    query, key_value = call(heads_kernel, (2, 4), (qkv_own, qkv_twin, q_gain, k_gain))
    (hidden,) = call(hidden_kernel, (6,), (up_own, up_twin, bias_own, bias_twin))
    return query, key_value, hidden


def attend_kernel(count, size, *refs):
    query_refs, own_refs, twin_refs = (refs[i * count : (i + 1) * count] for i in range(3))
    out_refs = refs[-count:]

    def image(some, m, at):
        return [
            ref[pl.ds((j * NX + m) * size, size), at : at + HEAD_DIM]
            for ref in some
            for j in range(ref.shape[0] // (NX * size))
        ]

    for m in range(NX):
        for t in range(2):
            own, twin = 2 * t * HEAD_DIM, 2 * (1 - t) * HEAD_DIM
            query = jnp.concatenate(image(query_refs, m, t * HEAD_DIM), axis=0)
            key_rows = jnp.concatenate(image(own_refs, m, own) + image(twin_refs, m, twin), axis=0)
            value = jnp.concatenate(
                image(own_refs, m, own + HEAD_DIM) + image(twin_refs, m, twin + HEAD_DIM), axis=0
            )
            scores = lax.dot_general(
                query, key_rows, (((1,), (1,)), ((), ())), preferred_element_type=F32
            )
            expo = jnp.exp(scores / math.sqrt(HEAD_DIM))
            weights = (expo / jnp.sum(expo, axis=-1, keepdims=True)).astype(BF16)
            mixed = dot(weights, value).astype(BF16)
            at = 0
            for ref in out_refs:
                for j in range(ref.shape[0] // (NX * size)):
                    ref[pl.ds((j * NX + m) * size, size), t * HEAD_DIM : (t + 1) * HEAD_DIM] = mixed[
                        at : at + size
                    ]
                    at += size


def attend(size, query, own, twin, first):
    return pl.pallas_call(
        functools.partial(attend_kernel, len(query), size),
        in_specs=whole(3 * len(query)) + [pl.BlockSpec(memory_space=pl.ANY)],
        out_specs=whole(len(query)),
        out_shape=[jax.ShapeDtypeStruct(a.shape, BF16) for a in query],
        compiler_params=pltpu.CompilerParams(vmem_limit_bytes=12 * MIB),
        cost_estimate=pl.CostEstimate(
            flops=140_000_000, bytes_accessed=2_000_000, transcendentals=270_000
        ),
    )(*query, *own, *twin, first)


def spread_kernel(start, att, hid, out_own, out_twin, *rest):
    outs = rest[-NX:]
    size = outs[0].shape[0]
    head = HEAD_DIM
    span = pl.ds(start, NX * size)
    left = jnp.concatenate(
        [att[span, :head], hid[span, : 3 * head], att[span, head:], hid[span, 3 * head :]], axis=1
    )
    right = jnp.concatenate([out_own[...], out_twin[...]], axis=0)
    partial = dot(left, right).astype(BF16)
    for m, out in enumerate(outs):
        out[...] = partial[m * size : (m + 1) * size]


def spread(size, start, att, hid, weights, first):
    depth = weights[0].shape[1]
    return pl.pallas_call(
        functools.partial(spread_kernel, start),
        in_specs=whole(4) + [pl.BlockSpec(memory_space=pl.ANY)] * len(first),
        out_specs=whole(NX),
        out_shape=[jax.ShapeDtypeStruct((size, depth), BF16)] * NX,
        compiler_params=pltpu.CompilerParams(vmem_limit_bytes=16 * MIB),
        cost_estimate=pl.CostEstimate(
            flops=16 * NX * size * depth * HEAD_DIM,
            bytes_accessed=16 * depth * HEAD_DIM + 2 * NX * size * depth,
            transcendentals=0,
        ),
    )(att, hid, *weights, *first)


def added(*parts):
    return sum(p.astype(F32) for p in parts).astype(BF16)


def shards(tokens, ln_gain, w_qkv, q_gain, k_gain, w_up, up_bias, w_out_attn, w_down):
    rows, depth = tokens.shape
    w_qkv = jnp.transpose(w_qkv, (1, 0, 2))
    up_twin, qkv_twin = send(w_up, TWIN), send(w_qkv, TWIN)

    held, left, right, far = {}, {}, {}, {}
    held[0] = norm_rows(tokens, ln_gain)
    next1 = send(held[0], UP)
    left[0] = send(held[0], RIGHT)
    right[0] = send(held[0], LEFT)
    held[1] = gate(next1, left[0], right[0], up_twin, qkv_twin)
    next2 = send(held[1], UP)
    far[0] = send(left[0], RIGHT)
    right[1] = send(held[1], LEFT)
    left[1] = send(held[1], RIGHT)
    far[1] = send(right[1], LEFT)
    held[2] = gate(next2, far[0], right[1])
    next3 = send(held[2], UP)
    left[2] = send(held[2], RIGHT)
    right[2] = send(held[2], LEFT)
    far[2] = send(left[2], RIGHT)
    held[3] = gate(next3, far[1], left[1], left[2], right[2])
    right[3] = send(held[3], LEFT)
    left[3] = send(held[3], RIGHT)
    bias_twin = send(pack(up_bias.shape, (left[1],), up_bias), TWIN)
    out_own = pack(
        (4 * HEAD_DIM, depth), (far[1], left[2], right[2], next3, bias_twin), w_out_attn, w_down
    )
    w_in = (w_qkv, qkv_twin, w_up, up_twin, q_gain, k_gain, up_bias, bias_twin)
    w_out = (out_own, send(out_own, TWIN))

    def rows_of(*blocks):
        return [a[k] for k in blocks for a in (held, left, right, far)]

    *early, kept = project(rows_of(0, 1), w_in, keep=True)
    half = rows // 2
    far_top = send(part(left[3], 0, half, early[0]), RIGHT)
    far_bottom = send(part(right[3], half, half, early[0]), LEFT)
    w_in = (w_qkv, kept, *w_in[2:])
    last = [held[3], left[3], right[3], far_top, far_bottom]
    query, own, hidden = zip(early, project(rows_of(2), w_in), project_in_two(last, *w_in))
    twin = [send(part, TWIN) for part in own]
    attended = attend(rows, query, own, twin, hidden[2])

    block_rows = NX * rows
    place = {0: (0, 0), 1: (0, block_rows), 2: (1, 0), 3: (2, 0)}

    def block_sums(k, *first):
        group, start = place[k]
        return spread(rows, start, attended[group], hidden[group], w_out, first)

    mine1, left1, right1, far1 = block_sums(1)
    far1 = send(far1, LEFT)
    from_left1 = send(right1, RIGHT)
    mine2, left2, right2, far2 = block_sums(2, mine1)
    far2 = send(far2, RIGHT)
    from_right1 = send(added(left1, far1), LEFT)
    from_right2 = send(left2, LEFT)
    from_left2 = send(added(right2, far2), RIGHT)
    mine3, left3, right3, far3 = block_sums(3, mine2, far2, far1)
    sum1 = added(mine1, from_left1, from_right1)
    up1 = send(sum1, UP)
    far3 = send(far3, LEFT)
    from_left3 = send(right3, RIGHT)
    mine0, left0, right0, far0 = block_sums(0, mine3)
    far0 = send(gate(far0, sum1), RIGHT)
    from_right3 = send(added(left3, far3), LEFT)
    up2 = send(added(mine2, from_left2, from_right2, up1), UP)
    from_right0 = send(gate(left0, up1), LEFT)
    from_left0 = send(added(right0, far0), RIGHT)
    up3 = send(added(mine3, from_left3, from_right3, up2), UP)
    return added(tokens, mine0, from_left0, from_right0, up3)


def solution(mesh):
    placed = (
        P(("dp", "mp"), None),
        P(),
        P(None, None, "mp"),
        P(),
        P(),
        P(None, "mp"),
        P("mp"),
        P("mp", None),
        P("mp", None),
    )
    return jax.shard_map(
        shards, mesh=mesh, in_specs=placed, out_specs=P(("dp", "mp"), None), check_vma=False
    )
```
